128 devices in a mesh: ty: 8 (over x, y_hi), tx: 16 (over z, y_lo, core).
Axes of the slice: x: 4, y: 4 (y_hi: 2, y_lo: 2; y = y_hi * 2 + y_lo), z: 4, core: 2. Of those that a mesh axis runs over, the one named last changes fastest.
Arguments:
- object_slices: bfloat16 [4, 2, 2048, 4096], P(None, None, 'ty', 'tx'), may hold values from -1 to 1, as said below
- probe_wave: float32 [2, 256, 256], replicated, may hold values from -4 to 4
- intensity: float32 [384, 256, 256], P(('ty', 'tx')), may hold values from 0.1 to 4
- offsets: int32 [384, 2], P(('ty', 'tx')), may hold values from 0 to 3840, as said below
- live_slots: int32 [384], P(('ty', 'tx')), may hold values from 0 to 1, as said below
- prop_phase: float32 [256, 256], replicated, may hold values from -3.140625 to 3.140625
Outputs:
- grad_object: float32 [4, 2, 2048, 4096], P(None, None, 'ty', 'tx')
The draws below stay inside these ranges and needn't reach their ends.
Inputs may be any that keep to these rules, and one draw needn't show every extreme that they name: `object_slices`: each complex entry has magnitude between 0.6 and 1. `offsets`: slot p belongs to device p // 3 of the mesh (ty slower, tx faster). On the device with tile (i, j) a slot's row offset lies in [i * 256 - 128, (i + 1) * 256 - 128) and its column offset in [j * 256 - 128, (j + 1) * 256 - 128), both further held within [0, 1792] and [0, 3840]; on every device both ends of each of these windows are taken by some slot. `live_slots`: on each device the live slots are its first ones, at least one; some device has all 3 live.
All inputs are finite; a program needn't handle non-finite values.
Results may differ from the reference program's by a relative error of at most 0.03.
Values may be sent and summed in bfloat16 or wider, within the bound.
A program may use at most 128 MiB of HBM per device.

```python
import math
import jax
import jax.numpy as jnp
from jax import lax

P_SIZE = 256
HALO = 128
SLICES = 4
TILE = 256
CAP = 3
NH = 2048
NW = 4096
POSITIONS = 384


def draw_object_slices(key, part):
    key = jax.random.fold_in(key, 13)
    keys = jax.random.split(key, 2)
    log_amp = jax.random.uniform(keys[0], (SLICES, NH, NW), jnp.float32, math.log(0.6), 0.0)
    phase = jax.random.uniform(keys[1], (SLICES, NH, NW), jnp.float32, -math.pi, math.pi)
    amp = jnp.exp(log_amp)
    return jnp.stack([amp * jnp.cos(phase), amp * jnp.sin(phase)], 1).astype(jnp.bfloat16)


def draw_offsets(key, part):
    key = jax.random.fold_in(key, 11)
    keys = jax.random.split(key, 4)
    device_count = POSITIONS // CAP
    tile_cols = NW // TILE
    position = jnp.arange(POSITIONS, dtype=jnp.int32)
    device = position // CAP
    slot_index = position % CAP
    tile_i = device // tile_cols
    tile_j = device % tile_cols
    row_draw = jax.random.randint(keys[0], (POSITIONS,), 0, TILE)
    col_draw = jax.random.randint(keys[1], (POSITIONS,), 0, TILE)
    row_pick = jax.random.randint(keys[2], (device_count,), 0, CAP)[device]
    col_pick = jax.random.randint(keys[3], (device_count,), 0, CAP)[device]
    row_draw = jnp.where(slot_index == row_pick, 0, row_draw)
    row_draw = jnp.where(slot_index == (row_pick + 1) % CAP, TILE - 1, row_draw)
    col_draw = jnp.where(slot_index == col_pick, TILE - 1, col_draw)
    col_draw = jnp.where(slot_index == (col_pick + 1) % CAP, 0, col_draw)
    row_off = jnp.clip(tile_i * TILE - HALO + row_draw, 0, NH - P_SIZE)
    col_off = jnp.clip(tile_j * TILE - HALO + col_draw, 0, NW - P_SIZE)
    return jnp.stack([row_off, col_off], 1).astype(jnp.int32)


def draw_live_slots(key, part):
    key = jax.random.fold_in(key, 12)
    keys = jax.random.split(key, 2)
    device_count = POSITIONS // CAP
    counts = jax.random.randint(keys[0], (device_count,), 1, CAP + 1)
    busiest = jax.random.randint(keys[1], (), 0, device_count)
    counts = jnp.where(jnp.arange(device_count) == busiest, CAP, counts)
    position = jnp.arange(POSITIONS, dtype=jnp.int32)
    return (position % CAP < counts[position // CAP]).astype(jnp.int32)


def levels(own_key, dims, cuts, smallest, largest):
    gain, own = 1.0, jax.random.fold_in(own_key, 6)
    for dim, parts in cuts:
        heights = jnp.exp(jax.random.uniform(jax.random.fold_in(own, dim), (parts,), jnp.float32, smallest / len(cuts), largest / len(cuts)))
        gain = gain * jnp.repeat(heights, dims[dim] // parts).reshape([-1 if axis == dim else 1 for axis in range(len(dims))])
    return gain


def bell_draw(own_key, dims, scale, limit, held_as=jnp.bfloat16):
    return jnp.clip(scale * jax.random.normal(own_key, dims, jnp.float32), -limit, limit).astype(held_as)


def setup_inputs(seed: int = 0) -> dict:
    key_list = jax.random.split(jax.random.key(seed), 7)
    object_slices = draw_object_slices(jax.random.fold_in(key_list[6], 71), 0)
    probe_wave = bell_draw(key_list[1], (2, P_SIZE, P_SIZE), 0.7, 4.0, jnp.float32)
    intensity = jnp.clip(jnp.exp(math.log(4.0) - 3.6888794 * jax.random.uniform(key_list[2], (POSITIONS, P_SIZE, P_SIZE), jnp.float32) ** levels(key_list[2], (POSITIONS, P_SIZE, P_SIZE), ((0, 128),), -0.2, 0.2)), 0.1, 4.0)
    offsets = draw_offsets(jax.random.fold_in(key_list[6], 71), 0)
    live_slots = draw_live_slots(jax.random.fold_in(key_list[6], 71), 0)
    prop_phase = jnp.clip(jax.random.uniform(key_list[5], (P_SIZE, P_SIZE), jnp.float32, -3.140625, 3.140625), -3.140625, 3.140625)
    return dict(object_slices=object_slices, probe_wave=probe_wave, intensity=intensity, offsets=offsets, live_slots=live_slots, prop_phase=prop_phase)


def dft_tables(probe_side):
    index = jnp.arange(probe_side, dtype=jnp.int32)
    product = index[:, None] * index[None, :] % probe_side
    angle = product.astype(jnp.float32) * (2.0 * math.pi / probe_side)
    cosine = jnp.cos(angle) / math.sqrt(probe_side)
    sine = jnp.sin(angle) / math.sqrt(probe_side)

    def block(upper):
        return jnp.stack([jnp.stack([cosine, upper], 1), jnp.stack([-upper, cosine], 1)], 0).astype(jnp.bfloat16)
    return (block(sine), block(-sine))

def transform(field, left_tab, right_tab):
    rounded = field.astype(jnp.bfloat16).astype(jnp.float32)
    middle = jnp.einsum('aibj,bjk->aik', left_tab.astype(jnp.float32), rounded)
    middle = middle.astype(jnp.bfloat16).astype(jnp.float32)
    return jnp.einsum('bik,bkal->ail', middle, right_tab.astype(jnp.float32))

def complex_mul(first, second):
    return jnp.stack([first[0] * second[0] - first[1] * second[1], first[0] * second[1] + first[1] * second[0]])

def exit_wave(patch_data, probe_wave, plus_tab, minus_tab, kernel):
    current = probe_wave
    slice_count = patch_data.shape[0]
    for layer in range(slice_count):
        product = complex_mul(current, patch_data[layer])
        if layer < slice_count - 1:
            spectrum = complex_mul(transform(product, plus_tab, minus_tab), kernel)
            current = transform(spectrum, minus_tab, plus_tab)
        else:
            current = transform(product, plus_tab, minus_tab)
    return current

def slot_grads(patch_data, probe_wave, measured, weight, plus_tab, minus_tab, kernel):

    def loss_of(patch_float):
        far_field = exit_wave(patch_float, probe_wave, plus_tab, minus_tab, kernel)
        power = far_field[0] * far_field[0] + far_field[1] * far_field[1]
        resid = (power - measured) * weight
        return 0.5 * jnp.sum(resid * resid)
    _, pull = jax.vjp(loss_of, patch_data.astype(jnp.float32))
    return pull(jnp.ones((), jnp.float32))[0]

def reference(object_slices, probe_wave, intensity, offsets, live_slots, prop_phase):
    slice_count = object_slices.shape[0]
    probe_side = probe_wave.shape[-1]
    plus_tab, minus_tab = dft_tables(probe_side)
    kernel = jnp.stack([jnp.cos(prop_phase), jnp.sin(prop_phase)])
    zero_index = jnp.zeros((), jnp.int32)
    window = (slice_count, 2, probe_side, probe_side)

    def step_one(grad_all, item):
        corner_pos, measured, flag = item
        start = (zero_index, zero_index, corner_pos[0].astype(jnp.int32), corner_pos[1].astype(jnp.int32))
        patch_data = lax.dynamic_slice(object_slices, start, window)
        grad_patch = slot_grads(patch_data, probe_wave, measured, flag.astype(jnp.float32), plus_tab, minus_tab, kernel)
        previous = lax.dynamic_slice(grad_all, start, window)
        grad_all = lax.dynamic_update_slice(grad_all, previous + grad_patch, start)
        return (grad_all, None)
    initial = jnp.zeros(object_slices.shape, jnp.float32)
    grad_all, _ = lax.scan(step_one, initial, (offsets, intensity, live_slots))
    return grad_all
```

```python
import functools
import math

import jax
import jax.numpy as jnp
import numpy as np
from jax import lax
from jax.experimental import pallas as pl
from jax.experimental.pallas import tpu as pltpu
from jax.sharding import PartitionSpec as P

MESH = pl.DeviceIdType.MESH
BF16 = jnp.bfloat16
F32 = jnp.float32
ROWS = 32


def dft_matrix(side):
    index = np.arange(side)
    angle = (index[:, None] * index[None, :] % side) * (2.0 * math.pi / side)
    parts = np.stack([np.cos(angle), -np.sin(angle)]) / math.sqrt(side)
    return parts.astype(np.float32).astype(jnp.bfloat16).astype(np.float32)


def dot(first, second):
    return jnp.dot(first, second, preferred_element_type=F32)


def kernel(
    grid,
    off,
    live,
    obj,
    probe,
    inten,
    phase,
    dft,
    out,
    pad,
    gpad,
    patch,
    wave,
    tl,
    tle,
    tr,
    tre,
    kern,
    ub,
    mb,
    xb,
    ct,
    yb,
    zb,
    gc,
    land_r,
    land_c,
    land_d,
    land_m,
    halo_send,
    halo_recv,
    grad_send,
    grad_recv,
):
    nty, ntx = grid
    slices, _, n, _ = obj.shape
    slots = inten.shape[0]
    h = n // 2
    ty, tx = lax.axis_index("ty"), lax.axis_index("tx")
    core = lax.rem(tx, 2)
    up, down = lax.rem(ty + nty - 1, nty), lax.rem(ty + 1, nty)
    left, right = lax.rem(tx + ntx - 1, ntx), lax.rem(tx + 1, ntx)
    far = lax.rem(tx + 2 * core - 1 + ntx, ntx)
    mate = tx + 1 - 2 * core
    targets = (
        (up, tx),
        (down, tx),
        (ty, left),
        (ty, right),
        (up, far),
        (down, far),
        (ty, mate),
        (ty, mate),
    )

    def blk(index):
        return pl.ds(pl.multiple_of(index * h, h), h)

    def halo(s, d):
        top, bottom = pl.ds(0, h), pl.ds(h, h)
        low, mid, high = pl.ds(0, h), pl.ds(h, n), pl.ds(3 * h, h)
        everything = slice(None)
        src, dst = (
            (obj.at[s, :, top, :], pad.at[s, :, high, mid]),
            (obj.at[s, :, bottom, :], pad.at[s, :, low, mid]),
            (obj.at[s, :, everything, top], pad.at[s, :, mid, high]),
            (obj.at[s, :, everything, bottom], pad.at[s, :, mid, low]),
            (obj.at[s, :, top, blk(core)], pad.at[s, :, high, blk(3 * (1 - core))]),
            (obj.at[s, :, bottom, blk(core)], pad.at[s, :, low, blk(3 * (1 - core))]),
            (pad.at[s, :, low, blk(2 - core)], pad.at[s, :, low, blk(3 * core)]),
            (pad.at[s, :, high, blk(2 - core)], pad.at[s, :, high, blk(3 * core)]),
        )[d]
        return pltpu.make_async_remote_copy(
            src_ref=src,
            dst_ref=dst,
            send_sem=halo_send.at[s, d],
            recv_sem=halo_recv.at[s, d],
            device_id=targets[d],
            device_id_type=MESH,
        )

    def back(s, d):
        low, mid, high = pl.ds(0, h), pl.ds(h, n), pl.ds(3 * h, h)
        src, dst = (
            (gpad.at[s, :, low, mid], land_r.at[s, 0]),
            (gpad.at[s, :, high, mid], land_r.at[s, 1]),
            (gpad.at[s, :, mid, low], land_c.at[s, 0]),
            (gpad.at[s, :, mid, high], land_c.at[s, 1]),
            (gpad.at[s, :, low, blk(3 * core)], land_d.at[s, 0]),
            (gpad.at[s, :, high, blk(3 * core)], land_d.at[s, 1]),
            (gpad.at[s, :, low, blk(3 * (1 - core))], land_m.at[s, 0]),
            (gpad.at[s, :, high, blk(3 * (1 - core))], land_m.at[s, 1]),
        )[d]
        return pltpu.make_async_remote_copy(
            src_ref=src,
            dst_ref=dst,
            send_sem=grad_send.at[s, d],
            recv_sem=grad_recv.at[s, d],
            device_id=targets[d],
            device_id_type=MESH,
        )

    barrier = pltpu.get_barrier_semaphore()
    for target in targets[:6]:
        pl.semaphore_signal(barrier, inc=1, device_id=target, device_id_type=MESH)
    pl.semaphore_wait(barrier, 6)

    for s in range(slices):
        for d in range(6):
            halo(s, d).start()

    def corner(k):
        return off[k, 0] - (ty * n - h), off[k, 1] - (tx * n - h)

    def masks(k, r):
        a, b = corner(k)
        row = lax.broadcasted_iota(jnp.int32, (ROWS, n), 0) + r >= a
        col = lax.broadcasted_iota(jnp.int32, (ROWS, n), 1) >= b
        return row, col

    chunks = range(0, n, ROWS)

    for s in range(slices):
        pad[s, :, h : h + n, h : h + n] = obj[s]
    for r in chunks:
        kern[0, r : r + ROWS, :] = jnp.cos(phase[r : r + ROWS, :])
        kern[1, r : r + ROWS, :] = jnp.sin(phase[r : r + ROWS, :])

    def prepare(k, carry):
        a, b = corner(k)
        for axis, shift, table, sign in (
            (1, a, tl, -1.0),
            (0, a, tle, 1.0),
            (0, b, tr, 1.0),
            (1, b, tre, -1.0),
        ):
            real = pltpu.roll(dft[0], shift, axis).astype(BF16)
            imag = pltpu.roll(dft[1], shift, axis)
            table[k, 0:n, 0:n] = real
            table[k, n:, n:] = real
            table[k, 0:n, n:] = (sign * imag).astype(BF16)
            table[k, n:, 0:n] = (-sign * imag).astype(BF16)
        for part in range(2):
            moved = pltpu.roll(pltpu.roll(probe[part], a, 0), b, 1)
            wave[k, 0, :, part * n : (part + 1) * n] = moved
        return carry

    lax.fori_loop(0, slots, prepare, 0)

    def illuminate(s, k):
        for r in chunks:
            row, col = masks(k, r)
            rows = slice(r, r + ROWS)
            below = slice(n + r, n + r + ROWS)
            parts = []
            for part in range(2):
                value = jnp.where(
                    row,
                    jnp.where(col, pad[s, part, rows, 0:n].astype(F32), pad[s, part, rows, n:].astype(F32)),
                    jnp.where(col, pad[s, part, below, 0:n].astype(F32), pad[s, part, below, n:].astype(F32)),
                )
                patch[k, s, part, rows, :] = value.astype(BF16)
                parts.append(value)
            pr, pi = parts
            wr, wi = wave[k, s, rows, 0:n], wave[k, s, rows, n:]
            ub[rows, :] = (wr * pr - wi * pi).astype(BF16)
            ub[below, :] = (wr * pi + wi * pr).astype(BF16)

    def transform(left_table, right_table):
        mb[:, 0:n] = dot(left_table[0:n, :], ub[...]).astype(BF16)
        mb[:, n:] = dot(left_table[n:, :], ub[...]).astype(BF16)
        return dot(mb[...], right_table[...])

    def adjoint(k, right_table, left_table):
        yb[0:n, :] = dot(ct[k], right_table[:, 0:n]).astype(BF16)
        yb[n:, :] = dot(ct[k], right_table[:, n:]).astype(BF16)
        zb[...] = dot(left_table[...], yb[...]).astype(BF16)

    def arrive(s):
        for d in (0, 1):
            halo(s, d).wait_recv()
        for d in (6, 7):
            halo(s, d).start()
        for d in (2, 3, 4, 5, 6, 7):
            halo(s, d).wait_recv()

    def forward(s, carry):
        arrive(s)

        def slot(k, carry):
            illuminate(s, k)
            xb[...] = transform(tl.at[k], tr.at[k])
            for r in chunks:
                rows = slice(r, r + ROWS)
                below = slice(n + r, n + r + ROWS)
                kr, ki = kern[0, rows, :], kern[1, rows, :]
                xr, xi = xb[rows, 0:n], xb[rows, n:]
                ub[rows, :] = (kr * xr - ki * xi).astype(BF16)
                ub[below, :] = (kr * xi + ki * xr).astype(BF16)
            wave[k, s + 1] = transform(tle.at[k], tre.at[k])
            return carry

        return lax.fori_loop(0, slots, slot, carry)

    last = slices - 1
    lax.fori_loop(0, last, forward, 0)
    arrive(last)

    def tops(s):
        for d, rows in ((0, pl.ds(0, h)), (1, pl.ds(3 * h, h))):
            back(s, 6 + d).wait_recv()
            for part in range(2):
                place = (s, part, rows, blk(2 - core))
                total = gpad[place].astype(F32) + land_m[s, d, part].astype(F32)
                gpad[place] = total.astype(BF16)
            back(s, d).start()

    def slot_back(s, k, onward):
        adjoint(k, tre.at[k], tle.at[k])
        for r in chunks:
            rows = slice(r, r + ROWS)
            below = slice(n + r, n + r + ROWS)
            zr, zi = zb[rows, :].astype(F32), zb[below, :].astype(F32)
            wr, wi = wave[k, s, rows, 0:n], wave[k, s, rows, n:]
            gc[k, 0, rows, :] = zr * wr + zi * wi
            gc[k, 1, rows, :] = zi * wr - zr * wi
            if onward:
                pr, pi = patch[k, s, 0, rows, :].astype(F32), patch[k, s, 1, rows, :].astype(F32)
                ct[k, rows, 0:n] = (zr * pr + zi * pi).astype(BF16)
                ct[k, rows, n:] = (zi * pr - zr * pi).astype(BF16)
        if onward:
            adjoint(k, tr.at[k], tl.at[k])
            for r in chunks:
                rows = slice(r, r + ROWS)
                below = slice(n + r, n + r + ROWS)
                zr, zi = zb[rows, :].astype(F32), zb[below, :].astype(F32)
                kr, ki = kern[0, rows, :], kern[1, rows, :]
                ct[k, rows, 0:n] = (kr * zr + ki * zi).astype(BF16)
                ct[k, rows, n:] = (kr * zi - ki * zr).astype(BF16)

    def combine(s):
        for part in range(2):
            for r in chunks:
                rows = slice(r, r + ROWS)
                sums = [[None, None], [None, None]]
                for k in range(slots):
                    row, col = masks(k, r)
                    value = gc[k, part, rows, :]
                    zero = jnp.zeros_like(value)
                    for p in range(2):
                        kept = jnp.where(row, value, zero) if p == 0 else jnp.where(row, zero, value)
                        for q in range(2):
                            term = jnp.where(col, kept, zero) if q == 0 else jnp.where(col, zero, kept)
                            sums[p][q] = term if k == 0 else sums[p][q] + term
                for p in range(2):
                    start = p * n + r
                    inside = h <= start < h + n
                    for q in range(2):
                        if not inside:
                            gpad[s, part, start : start + ROWS, q * n : (q + 1) * n] = sums[p][q].astype(BF16)
                            continue
                        place = slice(start - h, start - h + ROWS)
                        if q == 0:
                            gpad[s, part, start : start + ROWS, 0:h] = sums[p][q][:, 0:h].astype(BF16)
                            out[s, part, place, 0:h] = sums[p][q][:, h:]
                        else:
                            out[s, part, place, h:] = sums[p][q][:, 0:h]
                            gpad[s, part, start : start + ROWS, 3 * h :] = sums[p][q][:, h:].astype(BF16)

    def leave(s):
        for d in (6, 7, 4, 5, 2, 3):
            back(s, d).start()

    def exit_slot(k, carry):
        illuminate(last, k)
        xb[...] = transform(tl.at[k], tr.at[k])
        weight = live[k].astype(F32)
        for r in chunks:
            rows = slice(r, r + ROWS)
            er, ei = xb[rows, 0:n], xb[rows, n:]
            resid = (er * er + ei * ei - inten[k, rows, :]) * weight
            scale = 2.0 * weight * resid
            ct[k, rows, 0:n] = (scale * er).astype(BF16)
            ct[k, rows, n:] = (scale * ei).astype(BF16)
        return carry

    lax.fori_loop(0, slots, exit_slot, 0)

    def backward(t, carry):
        s = last - t

        def slot(k, carry):
            slot_back(s, k, True)

            @pl.when((k == 0) & (t > 0))
            def _():
                tops(s + 1)

            return carry

        lax.fori_loop(0, slots, slot, 0)
        combine(s)
        leave(s)
        return carry

    lax.fori_loop(0, last, backward, 0)

    def slot_first(k, carry):
        slot_back(0, k, False)

        @pl.when(k == 0)
        def _():
            tops(1)

        return carry

    lax.fori_loop(0, slots, slot_first, 0)
    combine(0)
    leave(0)
    tops(0)

    def collect(t, carry):
        s = last - t
        for d in range(6):
            back(s, d).wait_recv()
        for part in range(2):
            out[s, part, h:, :] = out[s, part, h:, :] + land_r[s, 0, part].astype(F32)
            out[s, part, 0:h, :] = out[s, part, 0:h, :] + land_r[s, 1, part].astype(F32)
            out[s, part, :, h:] = out[s, part, :, h:] + land_c[s, 0, part].astype(F32)
            out[s, part, :, 0:h] = out[s, part, :, 0:h] + land_c[s, 1, part].astype(F32)
            for d, rows in ((0, pl.ds(h, h)), (1, pl.ds(0, h))):
                place = (s, part, rows, blk(core))
                out[place] = out[place] + land_d[s, d, part].astype(F32)
        return carry

    lax.fori_loop(0, slices, collect, 0)

    def drain(s, carry):
        for d in range(8):
            halo(s, d).wait_send()
            back(s, d).wait_send()
        return carry

    lax.fori_loop(0, slices, drain, 0)


def per_device(grid, object_slices, probe_wave, intensity, offsets, live_slots, prop_phase):
    slices, _, n, _ = object_slices.shape
    slots = intensity.shape[0]
    h = n // 2
    vmem, smem = pl.BlockSpec(memory_space=pltpu.VMEM), pl.BlockSpec(memory_space=pltpu.SMEM)
    table = pltpu.VMEM((slots, 2 * n, 2 * n), BF16)
    return pl.pallas_call(
        functools.partial(kernel, grid),
        out_shape=jax.ShapeDtypeStruct(object_slices.shape, F32),
        in_specs=[smem, smem, vmem, vmem, vmem, vmem, vmem],
        out_specs=vmem,
        scratch_shapes=[
            pltpu.VMEM((slices, 2, 2 * n, 2 * n), BF16),
            pltpu.VMEM((slices, 2, 2 * n, 2 * n), BF16),
            pltpu.VMEM((slots, slices, 2, n, n), BF16),
            pltpu.VMEM((slots, slices, n, 2 * n), F32),
            table,
            table,
            table,
            table,
            pltpu.VMEM((2, n, n), F32),
            pltpu.VMEM((2 * n, n), BF16),
            pltpu.VMEM((n, 2 * n), BF16),
            pltpu.VMEM((n, 2 * n), F32),
            pltpu.VMEM((slots, n, 2 * n), BF16),
            pltpu.VMEM((2 * n, n), BF16),
            pltpu.VMEM((2 * n, n), BF16),
            pltpu.VMEM((slots, 2, n, n), F32),
            pltpu.VMEM((slices, 2, 2, h, n), BF16),
            pltpu.VMEM((slices, 2, 2, n, h), BF16),
            pltpu.VMEM((slices, 2, 2, h, h), BF16),
            pltpu.VMEM((slices, 2, 2, h, h), BF16),
            pltpu.SemaphoreType.DMA((slices, 8)),
            pltpu.SemaphoreType.DMA((slices, 8)),
            pltpu.SemaphoreType.DMA((slices, 8)),
            pltpu.SemaphoreType.DMA((slices, 8)),
        ],
        compiler_params=pltpu.CompilerParams(
            collective_id=0, has_side_effects=True, vmem_limit_bytes=56 * 1024 * 1024
        ),
    )(
        offsets,
        live_slots,
        object_slices,
        probe_wave,
        intensity,
        prop_phase,
        jnp.asarray(dft_matrix(n)),
    )


def solution(mesh):
    in_specs = (
        P(None, None, "ty", "tx"),
        P(),
        P(("ty", "tx"), None, None),
        P(("ty", "tx"), None),
        P(("ty", "tx")),
        P(),
    )
    out_specs = P(None, None, "ty", "tx")
    grid = (mesh.shape["ty"], mesh.shape["tx"])
    return jax.shard_map(
        functools.partial(per_device, grid),
        mesh=mesh,
        in_specs=in_specs,
        out_specs=out_specs,
        check_vma=False,
    )
```

```python
import functools
import math

import jax
import jax.numpy as jnp
import numpy as np
from jax import lax
from jax.experimental import pallas as pl
from jax.experimental.pallas import tpu as pltpu
from jax.sharding import PartitionSpec as P

MESH = pl.DeviceIdType.MESH
BF16 = jnp.bfloat16
F32 = jnp.float32
ROWS = 32


def dft_matrix(side):
    index = np.arange(side)
    angle = (index[:, None] * index[None, :] % side) * (2.0 * math.pi / side)
    parts = np.stack([np.cos(angle), -np.sin(angle)]) / math.sqrt(side)
    return parts.astype(np.float32).astype(jnp.bfloat16).astype(np.float32)


def dot(first, second):
    return jnp.dot(first, second, preferred_element_type=F32)


def kernel(
    grid,
    off,
    live,
    obj,
    probe_in,
    inten_in,
    phase_in,
    dft_in,
    out,
    probe,
    inten,
    phase,
    dft,
    pad,
    gpad,
    patch,
    wave,
    tl,
    tle,
    tr,
    tre,
    kern,
    ub,
    mb,
    xb,
    ct,
    yb,
    zb,
    gc,
    land_r,
    land_c,
    land_d,
    land_m,
    halo_send,
    halo_recv,
    grad_send,
    grad_recv,
    own_sem,
):
    nty, ntx = grid
    slices, _, n, _ = obj.shape
    slots = inten.shape[0]
    h = n // 2
    ty, tx = lax.axis_index("ty"), lax.axis_index("tx")
    core = lax.rem(tx, 2)
    up, down = lax.rem(ty + nty - 1, nty), lax.rem(ty + 1, nty)
    left, right = lax.rem(tx + ntx - 1, ntx), lax.rem(tx + 1, ntx)
    far = lax.rem(tx + 2 * core - 1 + ntx, ntx)
    mate = tx + 1 - 2 * core
    targets = (
        (up, tx),
        (up, tx),
        (down, tx),
        (down, tx),
        (ty, left),
        (ty, right),
        (up, far),
        (down, far),
        (ty, mate),
        (ty, mate),
    )
    low, mid, high = pl.ds(0, h), pl.ds(h, n), pl.ds(3 * h, h)

    def blk(index):
        return pl.ds(pl.multiple_of(index * h, h), h)

    def remote(src, dst, send_sem, recv_sem, target):
        return pltpu.make_async_remote_copy(
            src_ref=src,
            dst_ref=dst,
            send_sem=send_sem,
            recv_sem=recv_sem,
            device_id=target,
            device_id_type=MESH,
        )

    def halo(s, d):
        top, bottom = pl.ds(0, h), pl.ds(h, h)
        everything = slice(None)
        near, away = 1 - core, core
        src, dst = (
            (obj.at[s, :, top, blk(near)], pad.at[s, :, high, blk(1 + near)]),
            (obj.at[s, :, top, blk(away)], pad.at[s, :, high, blk(1 + away)]),
            (obj.at[s, :, bottom, blk(near)], pad.at[s, :, low, blk(1 + near)]),
            (obj.at[s, :, bottom, blk(away)], pad.at[s, :, low, blk(1 + away)]),
            (obj.at[s, :, everything, top], pad.at[s, :, mid, high]),
            (obj.at[s, :, everything, bottom], pad.at[s, :, mid, low]),
            (obj.at[s, :, top, blk(core)], pad.at[s, :, high, blk(3 * (1 - core))]),
            (obj.at[s, :, bottom, blk(core)], pad.at[s, :, low, blk(3 * (1 - core))]),
            (pad.at[s, :, low, blk(1 + near)], pad.at[s, :, low, blk(3 * core)]),
            (pad.at[s, :, high, blk(1 + near)], pad.at[s, :, high, blk(3 * core)]),
        )[d]
        return remote(src, dst, halo_send.at[s, d], halo_recv.at[s, d], targets[d])

    def back(s, d):
        near, away = 1 - core, core
        src, dst = (
            (gpad.at[s, :, low, blk(1 + near)], land_r.at[s, 0, :, :, blk(near)]),
            (gpad.at[s, :, low, blk(1 + away)], land_r.at[s, 0, :, :, blk(away)]),
            (gpad.at[s, :, high, blk(1 + near)], land_r.at[s, 1, :, :, blk(near)]),
            (gpad.at[s, :, high, blk(1 + away)], land_r.at[s, 1, :, :, blk(away)]),
            (gpad.at[s, :, mid, low], land_c.at[s, 0]),
            (gpad.at[s, :, mid, high], land_c.at[s, 1]),
            (gpad.at[s, :, low, blk(3 * core)], land_d.at[s, 0]),
            (gpad.at[s, :, high, blk(3 * core)], land_d.at[s, 1]),
            (gpad.at[s, :, low, blk(3 * (1 - core))], land_m.at[s, 0]),
            (gpad.at[s, :, high, blk(3 * (1 - core))], land_m.at[s, 1]),
        )[d]
        return remote(src, dst, grad_send.at[s, d], grad_recv.at[s, d], targets[d])

    own = [
        pltpu.make_async_copy(src, dst, own_sem.at[index])
        for index, (src, dst) in enumerate(
            ((dft_in, dft), (probe_in, probe), (phase_in, phase), (obj, pad.at[:, :, mid, mid]), (inten_in, inten))
        )
    ]

    barrier = pltpu.get_barrier_semaphore()
    for target in ((up, tx), (down, tx), (ty, left), (ty, right), (up, far), (down, far)):
        pl.semaphore_signal(barrier, inc=1, device_id=target, device_id_type=MESH)
    pl.semaphore_wait(barrier, 6)

    for s in range(slices):
        for d in (4, 5):
            halo(s, d).start()
    for s in range(slices):
        for d in (6, 7, 0, 2, 1, 3):
            halo(s, d).start()
    for copy in own:
        copy.start()

    def corner(k):
        return off[0, k] - (ty * n - h), off[1, k] - (tx * n - h)

    def masks(k, r):
        a, b = corner(k)
        row = lax.broadcasted_iota(jnp.int32, (ROWS, n), 0) + r >= a
        col = lax.broadcasted_iota(jnp.int32, (ROWS, n), 1) >= b
        return row, col

    chunks = range(0, n, ROWS)

    for copy in own[:3]:
        copy.wait()
    for r in chunks:
        kern[0, r : r + ROWS, :] = jnp.cos(phase[r : r + ROWS, :])
        kern[1, r : r + ROWS, :] = jnp.sin(phase[r : r + ROWS, :])

    def prepare(k, carry):
        a, b = corner(k)
        for axis, shift, table, sign in (
            (1, a, tl, -1.0),
            (0, a, tle, 1.0),
            (0, b, tr, 1.0),
            (1, b, tre, -1.0),
        ):
            real = pltpu.roll(dft[0], shift, axis).astype(BF16)
            imag = pltpu.roll(dft[1], shift, axis)
            table[k, 0:n, 0:n] = real
            table[k, n:, n:] = real
            table[k, 0:n, n:] = (sign * imag).astype(BF16)
            table[k, n:, 0:n] = (-sign * imag).astype(BF16)
        for part in range(2):
            moved = pltpu.roll(pltpu.roll(probe[part], a, 0), b, 1)
            wave[k, 0, :, part * n : (part + 1) * n] = moved
        return carry

    lax.fori_loop(0, slots, prepare, 0)
    for copy in own[3:]:
        copy.wait()

    def illuminate(s, k):
        for r in chunks:
            row, col = masks(k, r)
            rows = slice(r, r + ROWS)
            below = slice(n + r, n + r + ROWS)
            parts = []
            for part in range(2):
                value = jnp.where(
                    row,
                    jnp.where(col, pad[s, part, rows, 0:n].astype(F32), pad[s, part, rows, n:].astype(F32)),
                    jnp.where(col, pad[s, part, below, 0:n].astype(F32), pad[s, part, below, n:].astype(F32)),
                )
                patch[k, s, part, rows, :] = value.astype(BF16)
                parts.append(value)
            pr, pi = parts
            wr, wi = wave[k, s, rows, 0:n], wave[k, s, rows, n:]
            ub[k, rows, :] = (wr * pr - wi * pi).astype(BF16)
            ub[k, below, :] = (wr * pi + wi * pr).astype(BF16)

    def left_of(k, table):
        mb[k, :, 0:n] = dot(table[k, 0:n, :], ub[k]).astype(BF16)
        mb[k, :, n:] = dot(table[k, n:, :], ub[k]).astype(BF16)

    def propagate(k):
        for r in chunks:
            rows = slice(r, r + ROWS)
            below = slice(n + r, n + r + ROWS)
            kr, ki = kern[0, rows, :], kern[1, rows, :]
            xr, xi = xb[k, rows, 0:n], xb[k, rows, n:]
            ub[k, rows, :] = (kr * xr - ki * xi).astype(BF16)
            ub[k, below, :] = (kr * xi + ki * xr).astype(BF16)

    def residual(k):
        weight = live[k].astype(F32)
        for r in chunks:
            rows = slice(r, r + ROWS)
            er, ei = xb[k, rows, 0:n], xb[k, rows, n:]
            resid = (er * er + ei * ei - inten[k, rows, :]) * weight
            scale = 2.0 * weight * resid
            ct[k, rows, 0:n] = (scale * er).astype(BF16)
            ct[k, rows, n:] = (scale * ei).astype(BF16)

    def right_adjoint(k, table):
        yb[k, 0:n, :] = dot(ct[k], table[k, :, 0:n]).astype(BF16)
        yb[k, n:, :] = dot(ct[k], table[k, :, n:]).astype(BF16)

    def left_adjoint(k, table):
        zb[k] = dot(table[k], yb[k]).astype(BF16)

    def gradient(s, k, onward):
        for r in chunks:
            rows = slice(r, r + ROWS)
            below = slice(n + r, n + r + ROWS)
            zr, zi = zb[k, rows, :].astype(F32), zb[k, below, :].astype(F32)
            wr, wi = wave[k, s, rows, 0:n], wave[k, s, rows, n:]
            gc[k, 0, rows, :] = zr * wr + zi * wi
            gc[k, 1, rows, :] = zi * wr - zr * wi
            if onward:
                pr, pi = patch[k, s, 0, rows, :].astype(F32), patch[k, s, 1, rows, :].astype(F32)
                ct[k, rows, 0:n] = (zr * pr + zi * pi).astype(BF16)
                ct[k, rows, n:] = (zi * pr - zr * pi).astype(BF16)

    def propagate_adjoint(k):
        for r in chunks:
            rows = slice(r, r + ROWS)
            below = slice(n + r, n + r + ROWS)
            zr, zi = zb[k, rows, :].astype(F32), zb[k, below, :].astype(F32)
            kr, ki = kern[0, rows, :], kern[1, rows, :]
            ct[k, rows, 0:n] = (kr * zr + ki * zi).astype(BF16)
            ct[k, rows, n:] = (kr * zi - ki * zr).astype(BF16)

    def every(stage, *operands):
        for k in range(slots):
            stage(k, *operands)

    def arrive(s):
        for d in (0, 2):
            halo(s, d).wait_recv()
        for d in (8, 9):
            halo(s, d).start()
        for d in (1, 3, 4, 5, 6, 7, 8, 9):
            halo(s, d).wait_recv()

    def forward(s, carry):
        arrive(s)
        for k in range(slots):
            illuminate(s, k)
        every(left_of, tl)
        for k in range(slots):
            xb[k] = dot(mb[k], tr[k])
        every(propagate)
        every(left_of, tle)
        for k in range(slots):
            wave[k, s + 1] = dot(mb[k], tre[k])
        return carry

    last = slices - 1
    lax.fori_loop(0, last, forward, 0)
    arrive(last)

    def tops(s):
        for d, rows in ((0, pl.ds(0, h)), (1, pl.ds(3 * h, h))):
            back(s, 8 + d).wait_recv()
            for part in range(2):
                place = (s, part, rows, blk(2 - core))
                total = gpad[place].astype(F32) + land_m[s, d, part].astype(F32)
                gpad[place] = total.astype(BF16)
            back(s, 2 * d).start()

    def combine(s):
        for part in range(2):
            for r in chunks:
                rows = slice(r, r + ROWS)
                sums = [[None, None], [None, None]]
                for k in range(slots):
                    row, col = masks(k, r)
                    value = gc[k, part, rows, :]
                    zero = jnp.zeros_like(value)
                    for p in range(2):
                        kept = jnp.where(row, value, zero) if p == 0 else jnp.where(row, zero, value)
                        for q in range(2):
                            term = jnp.where(col, kept, zero) if q == 0 else jnp.where(col, zero, kept)
                            sums[p][q] = term if k == 0 else sums[p][q] + term
                for p in range(2):
                    start = p * n + r
                    inside = h <= start < h + n
                    for q in range(2):
                        if not inside:
                            gpad[s, part, start : start + ROWS, q * n : (q + 1) * n] = sums[p][q].astype(BF16)
                            continue
                        place = slice(start - h, start - h + ROWS)
                        if q == 0:
                            gpad[s, part, start : start + ROWS, 0:h] = sums[p][q][:, 0:h].astype(BF16)
                            out[s, part, place, 0:h] = sums[p][q][:, h:]
                        else:
                            out[s, part, place, h:] = sums[p][q][:, 0:h]
                            gpad[s, part, start : start + ROWS, 3 * h :] = sums[p][q][:, h:].astype(BF16)

    def leave(s):
        for d in (8, 9, 4, 5, 6, 7, 1, 3):
            back(s, d).start()

    for k in range(slots):
        illuminate(last, k)
    every(left_of, tl)
    for k in range(slots):
        xb[k] = dot(mb[k], tr[k])
    every(residual)

    def backward(t, carry):
        s = last - t
        every(right_adjoint, tre)
        every(left_adjoint, tle)

        @pl.when(t > 0)
        def _():
            tops(s + 1)

        for k in range(slots):
            gradient(s, k, True)
        combine(s)
        leave(s)
        every(right_adjoint, tr)
        every(left_adjoint, tl)
        every(propagate_adjoint)
        return carry

    lax.fori_loop(0, last, backward, 0)
    every(right_adjoint, tre)
    every(left_adjoint, tle)
    tops(1)
    for k in range(slots):
        gradient(0, k, False)
    combine(0)
    leave(0)
    tops(0)

    def collect(t, carry):
        s = last - t
        for d in range(8):
            back(s, d).wait_recv()
        for part in range(2):
            out[s, part, h:, :] = out[s, part, h:, :] + land_r[s, 0, part].astype(F32)
            out[s, part, 0:h, :] = out[s, part, 0:h, :] + land_r[s, 1, part].astype(F32)
            out[s, part, :, h:] = out[s, part, :, h:] + land_c[s, 0, part].astype(F32)
            out[s, part, :, 0:h] = out[s, part, :, 0:h] + land_c[s, 1, part].astype(F32)
            for d, rows in ((0, pl.ds(h, h)), (1, pl.ds(0, h))):
                place = (s, part, rows, blk(core))
                out[place] = out[place] + land_d[s, d, part].astype(F32)
        return carry

    lax.fori_loop(0, slices, collect, 0)

    def drain(s, carry):
        for d in range(10):
            halo(s, d).wait_send()
            back(s, d).wait_send()
        return carry

    lax.fori_loop(0, slices, drain, 0)


def per_device(grid, object_slices, probe_wave, intensity, offsets, live_slots, prop_phase):
    slices, _, n, _ = object_slices.shape
    slots = intensity.shape[0]
    h = n // 2
    vmem, smem = pl.BlockSpec(memory_space=pltpu.VMEM), pl.BlockSpec(memory_space=pltpu.SMEM)
    table = pltpu.VMEM((slots, 2 * n, 2 * n), BF16)
    return pl.pallas_call(
        functools.partial(kernel, grid),
        out_shape=pltpu.VMEM(object_slices.shape, F32),
        in_specs=[smem, smem] + [pl.BlockSpec(memory_space=pl.ANY)] * 5,
        out_specs=vmem,
        scratch_shapes=[
            pltpu.VMEM(probe_wave.shape, F32),
            pltpu.VMEM(intensity.shape, F32),
            pltpu.VMEM(prop_phase.shape, F32),
            pltpu.VMEM((2, n, n), F32),
            pltpu.VMEM((slices, 2, 2 * n, 2 * n), BF16),
            pltpu.VMEM((slices, 2, 2 * n, 2 * n), BF16),
            pltpu.VMEM((slots, slices, 2, n, n), BF16),
            pltpu.VMEM((slots, slices, n, 2 * n), F32),
            table,
            table,
            table,
            table,
            pltpu.VMEM((2, n, n), F32),
            pltpu.VMEM((slots, 2 * n, n), BF16),
            pltpu.VMEM((slots, n, 2 * n), BF16),
            pltpu.VMEM((slots, n, 2 * n), F32),
            pltpu.VMEM((slots, n, 2 * n), BF16),
            pltpu.VMEM((slots, 2 * n, n), BF16),
            pltpu.VMEM((slots, 2 * n, n), BF16),
            pltpu.VMEM((slots, 2, n, n), F32),
            pltpu.VMEM((slices, 2, 2, h, n), BF16),
            pltpu.VMEM((slices, 2, 2, n, h), BF16),
            pltpu.VMEM((slices, 2, 2, h, h), BF16),
            pltpu.VMEM((slices, 2, 2, h, h), BF16),
            pltpu.SemaphoreType.DMA((slices, 10)),
            pltpu.SemaphoreType.DMA((slices, 10)),
            pltpu.SemaphoreType.DMA((slices, 10)),
            pltpu.SemaphoreType.DMA((slices, 10)),
            pltpu.SemaphoreType.DMA((5,)),
        ],
        compiler_params=pltpu.CompilerParams(
            collective_id=0, has_side_effects=True, vmem_limit_bytes=56 * 1024 * 1024
        ),
    )(
        offsets.T,
        live_slots,
        object_slices,
        probe_wave,
        intensity,
        prop_phase,
        jnp.asarray(dft_matrix(n)),
    )


def solution(mesh):
    in_specs = (
        P(None, None, "ty", "tx"),
        P(),
        P(("ty", "tx"), None, None),
        P(("ty", "tx"), None),
        P(("ty", "tx")),
        P(),
    )
    out_specs = P(None, None, "ty", "tx")
    grid = (mesh.shape["ty"], mesh.shape["tx"])
    return jax.shard_map(
        functools.partial(per_device, grid),
        mesh=mesh,
        in_specs=in_specs,
        out_specs=out_specs,
        check_vma=False,
    )
```

```python
import functools
import math

import jax
import jax.numpy as jnp
import numpy as np
from jax import lax
from jax.experimental import pallas as pl
from jax.experimental.pallas import tpu as pltpu
from jax.sharding import PartitionSpec as P

MESH = pl.DeviceIdType.MESH
BF16 = jnp.bfloat16
F32 = jnp.float32
ROWS = 32


def dft_matrix(side):
    index = np.arange(side)
    angle = (index[:, None] * index[None, :] % side) * (2.0 * math.pi / side)
    parts = np.stack([np.cos(angle), -np.sin(angle)]) / math.sqrt(side)
    return parts.astype(np.float32).astype(jnp.bfloat16).astype(np.float32)


def dot(first, second):
    return jnp.dot(first, second, preferred_element_type=F32)


def kernel(
    grid,
    off,
    live,
    obj,
    probe_in,
    inten_in,
    phase_in,
    dft_in,
    out,
    probe,
    inten,
    phase,
    dft,
    pad,
    gpad,
    patch,
    wave,
    tl,
    tle,
    tr,
    tre,
    kern,
    ub,
    mb,
    xb,
    ct,
    yb,
    zb,
    gc,
    land_r,
    land_c,
    land_d,
    land_m,
    halo_send,
    halo_recv,
    grad_send,
    grad_recv,
    own_sem,
):
    nty, ntx = grid
    slices, _, n, _ = obj.shape
    slots = inten.shape[0]
    h = n // 2
    ty, tx = lax.axis_index("ty"), lax.axis_index("tx")
    core = lax.rem(tx, 2)
    up, down = lax.rem(ty + nty - 1, nty), lax.rem(ty + 1, nty)
    left, right = lax.rem(tx + ntx - 1, ntx), lax.rem(tx + 1, ntx)
    far = lax.rem(tx + 2 * core - 1 + ntx, ntx)
    mate = tx + 1 - 2 * core
    targets = (
        (up, tx),
        (up, tx),
        (down, tx),
        (down, tx),
        (ty, left),
        (ty, right),
        (up, far),
        (down, far),
        (ty, mate),
        (ty, mate),
    )
    has_up, has_down, has_left, has_right = ty > 0, ty < nty - 1, tx > 0, tx < ntx - 1
    has_far = ((core == 0) & has_left) | ((core == 1) & has_right)
    sends = (
        has_up,
        has_up,
        has_down,
        has_down,
        has_left,
        has_right,
        has_up & has_far,
        has_down & has_far,
        has_up,
        has_down,
    )
    gets = (
        has_down,
        has_down,
        has_up,
        has_up,
        has_right,
        has_left,
        has_down & has_far,
        has_up & has_far,
        has_up,
        has_down,
    )

    def start(way, s, ds):
        for d in ds:
            pl.when(sends[d])(way(s, d).start)

    def await_arrival(way, s, ds):
        for d in ds:
            pl.when(gets[d])(way(s, d).wait_recv)

    def await_departure(way, s, ds):
        for d in ds:
            pl.when(sends[d])(way(s, d).wait_send)

    low, mid, high = pl.ds(0, h), pl.ds(h, n), pl.ds(3 * h, h)

    def blk(index):
        return pl.ds(pl.multiple_of(index * h, h), h)

    def remote(src, dst, send_sem, recv_sem, target):
        return pltpu.make_async_remote_copy(
            src_ref=src,
            dst_ref=dst,
            send_sem=send_sem,
            recv_sem=recv_sem,
            device_id=target,
            device_id_type=MESH,
        )

    def halo(s, d):
        top, bottom = pl.ds(0, h), pl.ds(h, h)
        everything = slice(None)
        near, away = 1 - core, core
        src, dst = (
            (obj.at[s, :, top, blk(near)], pad.at[s, :, high, blk(1 + near)]),
            (obj.at[s, :, top, blk(away)], pad.at[s, :, high, blk(1 + away)]),
            (obj.at[s, :, bottom, blk(near)], pad.at[s, :, low, blk(1 + near)]),
            (obj.at[s, :, bottom, blk(away)], pad.at[s, :, low, blk(1 + away)]),
            (obj.at[s, :, everything, top], pad.at[s, :, mid, high]),
            (obj.at[s, :, everything, bottom], pad.at[s, :, mid, low]),
            (obj.at[s, :, top, blk(core)], pad.at[s, :, high, blk(3 * (1 - core))]),
            (obj.at[s, :, bottom, blk(core)], pad.at[s, :, low, blk(3 * (1 - core))]),
            (pad.at[s, :, low, blk(1 + near)], pad.at[s, :, low, blk(3 * core)]),
            (pad.at[s, :, high, blk(1 + near)], pad.at[s, :, high, blk(3 * core)]),
        )[d]
        return remote(src, dst, halo_send.at[s, d], halo_recv.at[s, d], targets[d])

    def back(s, d):
        near, away = 1 - core, core
        src, dst = (
            (gpad.at[s, :, low, blk(1 + near)], land_r.at[s, 0, :, :, blk(near)]),
            (gpad.at[s, :, low, blk(1 + away)], land_r.at[s, 0, :, :, blk(away)]),
            (gpad.at[s, :, high, blk(1 + near)], land_r.at[s, 1, :, :, blk(near)]),
            (gpad.at[s, :, high, blk(1 + away)], land_r.at[s, 1, :, :, blk(away)]),
            (gpad.at[s, :, mid, low], land_c.at[s, 0]),
            (gpad.at[s, :, mid, high], land_c.at[s, 1]),
            (gpad.at[s, :, low, blk(3 * core)], land_d.at[s, 0]),
            (gpad.at[s, :, high, blk(3 * core)], land_d.at[s, 1]),
            (gpad.at[s, :, low, blk(3 * (1 - core))], land_m.at[s, 0]),
            (gpad.at[s, :, high, blk(3 * (1 - core))], land_m.at[s, 1]),
        )[d]
        return remote(src, dst, grad_send.at[s, d], grad_recv.at[s, d], targets[d])

    own = [
        pltpu.make_async_copy(src, dst, own_sem.at[index])
        for index, (src, dst) in enumerate(
            ((dft_in, dft), (probe_in, probe), (phase_in, phase), (obj, pad.at[:, :, mid, mid]), (inten_in, inten))
        )
    ]

    barrier = pltpu.get_barrier_semaphore()
    for d in (0, 2, 4, 5, 6, 7):

        @pl.when(sends[d])
        def _(d=d):
            pl.semaphore_signal(barrier, inc=1, device_id=targets[d], device_id_type=MESH)

    pl.semaphore_wait(barrier, sum(sends[d].astype(jnp.int32) for d in (0, 2, 4, 5, 6, 7)))

    for s in range(slices):
        start(halo, s, (4, 5))
    for s in range(slices):
        start(halo, s, (6, 7, 0, 2, 1, 3))
    for copy in own:
        copy.start()

    def corner(k):
        return off[0, k] - (ty * n - h), off[1, k] - (tx * n - h)

    def masks(k, r):
        a, b = corner(k)
        row = lax.broadcasted_iota(jnp.int32, (ROWS, n), 0) + r >= a
        col = lax.broadcasted_iota(jnp.int32, (ROWS, n), 1) >= b
        return row, col

    chunks = range(0, n, ROWS)

    for copy in own[:3]:
        copy.wait()
    for r in chunks:
        kern[0, r : r + ROWS, :] = jnp.cos(phase[r : r + ROWS, :])
        kern[1, r : r + ROWS, :] = jnp.sin(phase[r : r + ROWS, :])

    def prepare(k, carry):
        a, b = corner(k)
        for axis, shift, table, sign in (
            (1, a, tl, -1.0),
            (0, a, tle, 1.0),
            (0, b, tr, 1.0),
            (1, b, tre, -1.0),
        ):
            real = pltpu.roll(dft[0], shift, axis).astype(BF16)
            imag = pltpu.roll(dft[1], shift, axis)
            table[k, 0:n, 0:n] = real
            table[k, n:, n:] = real
            table[k, 0:n, n:] = (sign * imag).astype(BF16)
            table[k, n:, 0:n] = (-sign * imag).astype(BF16)
        for part in range(2):
            moved = pltpu.roll(pltpu.roll(probe[part], a, 0), b, 1)
            wave[k, 0, :, part * n : (part + 1) * n] = moved
        return carry

    lax.fori_loop(0, slots, prepare, 0)
    for copy in own[3:]:
        copy.wait()

    def illuminate(s, k):
        for r in chunks:
            row, col = masks(k, r)
            rows = slice(r, r + ROWS)
            below = slice(n + r, n + r + ROWS)
            parts = []
            for part in range(2):
                value = jnp.where(
                    row,
                    jnp.where(col, pad[s, part, rows, 0:n].astype(F32), pad[s, part, rows, n:].astype(F32)),
                    jnp.where(col, pad[s, part, below, 0:n].astype(F32), pad[s, part, below, n:].astype(F32)),
                )
                patch[k, s, part, rows, :] = value.astype(BF16)
                parts.append(value)
            pr, pi = parts
            wr, wi = wave[k, s, rows, 0:n], wave[k, s, rows, n:]
            ub[k, rows, :] = (wr * pr - wi * pi).astype(BF16)
            ub[k, below, :] = (wr * pi + wi * pr).astype(BF16)

    def left_of(k, table):
        mb[k, :, 0:n] = dot(table[k, 0:n, :], ub[k]).astype(BF16)
        mb[k, :, n:] = dot(table[k, n:, :], ub[k]).astype(BF16)

    def propagate(k):
        for r in chunks:
            rows = slice(r, r + ROWS)
            below = slice(n + r, n + r + ROWS)
            kr, ki = kern[0, rows, :], kern[1, rows, :]
            xr, xi = xb[k, rows, 0:n], xb[k, rows, n:]
            ub[k, rows, :] = (kr * xr - ki * xi).astype(BF16)
            ub[k, below, :] = (kr * xi + ki * xr).astype(BF16)

    def residual(k):
        weight = live[k].astype(F32)
        for r in chunks:
            rows = slice(r, r + ROWS)
            er, ei = xb[k, rows, 0:n], xb[k, rows, n:]
            resid = (er * er + ei * ei - inten[k, rows, :]) * weight
            scale = 2.0 * weight * resid
            ct[k, rows, 0:n] = (scale * er).astype(BF16)
            ct[k, rows, n:] = (scale * ei).astype(BF16)

    def right_adjoint(k, table):
        yb[k, 0:n, :] = dot(ct[k], table[k, :, 0:n]).astype(BF16)
        yb[k, n:, :] = dot(ct[k], table[k, :, n:]).astype(BF16)

    def left_adjoint(k, table):
        zb[k] = dot(table[k], yb[k]).astype(BF16)

    def gradient(s, k, onward):
        for r in chunks:
            rows = slice(r, r + ROWS)
            below = slice(n + r, n + r + ROWS)
            zr, zi = zb[k, rows, :].astype(F32), zb[k, below, :].astype(F32)
            wr, wi = wave[k, s, rows, 0:n], wave[k, s, rows, n:]
            gc[k, 0, rows, :] = zr * wr + zi * wi
            gc[k, 1, rows, :] = zi * wr - zr * wi
            if onward:
                pr, pi = patch[k, s, 0, rows, :].astype(F32), patch[k, s, 1, rows, :].astype(F32)
                ct[k, rows, 0:n] = (zr * pr + zi * pi).astype(BF16)
                ct[k, rows, n:] = (zi * pr - zr * pi).astype(BF16)

    def propagate_adjoint(k):
        for r in chunks:
            rows = slice(r, r + ROWS)
            below = slice(n + r, n + r + ROWS)
            zr, zi = zb[k, rows, :].astype(F32), zb[k, below, :].astype(F32)
            kr, ki = kern[0, rows, :], kern[1, rows, :]
            ct[k, rows, 0:n] = (kr * zr + ki * zi).astype(BF16)
            ct[k, rows, n:] = (kr * zi - ki * zr).astype(BF16)

    def every(stage, *operands):
        for k in range(slots):
            stage(k, *operands)

    def arrive(s):
        await_arrival(halo, s, (0, 2))
        start(halo, s, (8, 9))
        await_arrival(halo, s, (1, 3, 4, 5, 6, 7, 8, 9))

    def forward(s, carry):
        arrive(s)
        for k in range(slots):
            illuminate(s, k)
        every(left_of, tl)
        for k in range(slots):
            xb[k] = dot(mb[k], tr[k])
        every(propagate)
        every(left_of, tle)
        for k in range(slots):
            wave[k, s + 1] = dot(mb[k], tre[k])
        return carry

    last = slices - 1
    lax.fori_loop(0, last, forward, 0)
    arrive(last)

    def tops(s):
        for d, rows in ((0, low), (1, high)):

            @pl.when(gets[8 + d])
            def _(d=d, rows=rows):
                back(s, 8 + d).wait_recv()
                for part in range(2):
                    place = (s, part, rows, blk(2 - core))
                    total = gpad[place].astype(F32) + land_m[s, d, part].astype(F32)
                    gpad[place] = total.astype(BF16)
                back(s, 2 * d).start()

    def combine(s):
        for part in range(2):
            for r in chunks:
                rows = slice(r, r + ROWS)
                sums = [[None, None], [None, None]]
                for k in range(slots):
                    row, col = masks(k, r)
                    value = gc[k, part, rows, :]
                    zero = jnp.zeros_like(value)
                    for p in range(2):
                        kept = jnp.where(row, value, zero) if p == 0 else jnp.where(row, zero, value)
                        for q in range(2):
                            term = jnp.where(col, kept, zero) if q == 0 else jnp.where(col, zero, kept)
                            sums[p][q] = term if k == 0 else sums[p][q] + term
                for p in range(2):
                    start = p * n + r
                    inside = h <= start < h + n
                    for q in range(2):
                        if not inside:
                            gpad[s, part, start : start + ROWS, q * n : (q + 1) * n] = sums[p][q].astype(BF16)
                            continue
                        place = slice(start - h, start - h + ROWS)
                        if q == 0:
                            gpad[s, part, start : start + ROWS, 0:h] = sums[p][q][:, 0:h].astype(BF16)
                            out[s, part, place, 0:h] = sums[p][q][:, h:]
                        else:
                            out[s, part, place, h:] = sums[p][q][:, 0:h]
                            gpad[s, part, start : start + ROWS, 3 * h :] = sums[p][q][:, h:].astype(BF16)

    def sides(s):
        start(back, s, (8, 9, 4, 5, 6, 7))

    def rows_out(s):
        start(back, s, (1, 3))
        tops(s)

    for k in range(slots):
        illuminate(last, k)
    every(left_of, tl)
    for k in range(slots):
        xb[k] = dot(mb[k], tr[k])
    every(residual)

    def backward(t, carry):
        s = last - t
        every(right_adjoint, tre)
        every(left_adjoint, tle)
        for k in range(slots):
            gradient(s, k, True)
        combine(s)
        sides(s)

        @pl.when(t > 1)
        def _():
            rows_out(s + 1)

        @pl.when(t == 0)
        def _():
            start(back, s, (1, 3))

        every(right_adjoint, tr)

        @pl.when(t == 0)
        def _():
            tops(s)

        every(left_adjoint, tl)
        every(propagate_adjoint)
        return carry

    lax.fori_loop(0, last, backward, 0)
    every(right_adjoint, tre)
    every(left_adjoint, tle)
    for k in range(slots):
        gradient(0, k, False)
    combine(0)
    sides(0)
    rows_out(1)
    rows_out(0)

    def collect(t, carry):
        s = last - t
        whole, first, second = pl.ds(0, n), pl.ds(0, h), pl.ds(h, h)
        for ds, landed, rows, cols in (
            ((4,), land_c.at[s, 0], whole, second),
            ((5,), land_c.at[s, 1], whole, first),
            ((6,), land_d.at[s, 0], second, blk(core)),
            ((7,), land_d.at[s, 1], first, blk(core)),
            ((0, 1), land_r.at[s, 0], second, whole),
            ((2, 3), land_r.at[s, 1], first, whole),
        ):

            @pl.when(gets[ds[0]])
            def _(ds=ds, landed=landed, rows=rows, cols=cols):
                for d in ds:
                    back(s, d).wait_recv()
                for part in range(2):
                    place = (s, part, rows, cols)
                    out[place] = out[place] + landed[part].astype(F32)

        return carry

    lax.fori_loop(0, slices, collect, 0)

    def drain(s, carry):
        await_departure(halo, s, range(10))
        await_departure(back, s, range(10))
        return carry

    lax.fori_loop(0, slices, drain, 0)


def per_device(grid, object_slices, probe_wave, intensity, offsets, live_slots, prop_phase):
    slices, _, n, _ = object_slices.shape
    slots = intensity.shape[0]
    h = n // 2
    vmem, smem = pl.BlockSpec(memory_space=pltpu.VMEM), pl.BlockSpec(memory_space=pltpu.SMEM)
    table = pltpu.VMEM((slots, 2 * n, 2 * n), BF16)
    return pl.pallas_call(
        functools.partial(kernel, grid),
        out_shape=pltpu.VMEM(object_slices.shape, F32),
        in_specs=[smem, smem] + [pl.BlockSpec(memory_space=pl.ANY)] * 5,
        out_specs=vmem,
        scratch_shapes=[
            pltpu.VMEM(probe_wave.shape, F32),
            pltpu.VMEM(intensity.shape, F32),
            pltpu.VMEM(prop_phase.shape, F32),
            pltpu.VMEM((2, n, n), F32),
            pltpu.VMEM((slices, 2, 2 * n, 2 * n), BF16),
            pltpu.VMEM((slices, 2, 2 * n, 2 * n), BF16),
            pltpu.VMEM((slots, slices, 2, n, n), BF16),
            pltpu.VMEM((slots, slices, n, 2 * n), F32),
            table,
            table,
            table,
            table,
            pltpu.VMEM((2, n, n), F32),
            pltpu.VMEM((slots, 2 * n, n), BF16),
            pltpu.VMEM((slots, n, 2 * n), BF16),
            pltpu.VMEM((slots, n, 2 * n), F32),
            pltpu.VMEM((slots, n, 2 * n), BF16),
            pltpu.VMEM((slots, 2 * n, n), BF16),
            pltpu.VMEM((slots, 2 * n, n), BF16),
            pltpu.VMEM((slots, 2, n, n), F32),
            pltpu.VMEM((slices, 2, 2, h, n), BF16),
            pltpu.VMEM((slices, 2, 2, n, h), BF16),
            pltpu.VMEM((slices, 2, 2, h, h), BF16),
            pltpu.VMEM((slices, 2, 2, h, h), BF16),
            pltpu.SemaphoreType.DMA((slices, 10)),
            pltpu.SemaphoreType.DMA((slices, 10)),
            pltpu.SemaphoreType.DMA((slices, 10)),
            pltpu.SemaphoreType.DMA((slices, 10)),
            pltpu.SemaphoreType.DMA((5,)),
        ],
        compiler_params=pltpu.CompilerParams(
            collective_id=0, has_side_effects=True, vmem_limit_bytes=56 * 1024 * 1024
        ),
    )(
        offsets.T,
        live_slots,
        object_slices,
        probe_wave,
        intensity,
        prop_phase,
        jnp.asarray(dft_matrix(n)),
    )


def solution(mesh):
    in_specs = (
        P(None, None, "ty", "tx"),
        P(),
        P(("ty", "tx"), None, None),
        P(("ty", "tx"), None),
        P(("ty", "tx")),
        P(),
    )
    out_specs = P(None, None, "ty", "tx")
    grid = (mesh.shape["ty"], mesh.shape["tx"])
    return jax.shard_map(
        functools.partial(per_device, grid),
        mesh=mesh,
        in_specs=in_specs,
        out_specs=out_specs,
        check_vma=False,
    )
```

```python
import functools
import math

import jax
import jax.numpy as jnp
import numpy as np
from jax import lax
from jax.experimental import pallas as pl
from jax.experimental.pallas import tpu as pltpu
from jax.sharding import PartitionSpec as P

MESH = pl.DeviceIdType.MESH
BF16 = jnp.bfloat16
F32 = jnp.float32
ROWS = 32


def dft_matrix(side):
    index = np.arange(side)
    angle = (index[:, None] * index[None, :] % side) * (2.0 * math.pi / side)
    parts = np.stack([np.cos(angle), -np.sin(angle)]) / math.sqrt(side)
    return parts.astype(np.float32).astype(jnp.bfloat16).astype(np.float32)


def dot(first, second):
    return jnp.dot(first, second, preferred_element_type=F32)


def kernel(
    grid,
    off,
    live,
    obj,
    probe_in,
    inten_in,
    phase_in,
    dft_in,
    out,
    probe,
    inten,
    phase,
    dft,
    pad,
    gpad,
    patch,
    wave,
    tl,
    tle,
    tr,
    tre,
    kern,
    ub,
    mb,
    xb,
    ct,
    yb,
    zb,
    gc,
    land_r,
    land_c,
    land_d,
    land_m,
    halo_send,
    halo_recv,
    grad_send,
    grad_recv,
    own_sem,
    stage,
    first_send,
    first_recv,
    second_send,
):
    nty, ntx = grid
    slices, _, n, _ = obj.shape
    slots = inten.shape[0]
    h = n // 2
    ty, tx = lax.axis_index("ty"), lax.axis_index("tx")
    core = lax.rem(tx, 2)
    up, down = lax.rem(ty + nty - 1, nty), lax.rem(ty + 1, nty)
    left, right = lax.rem(tx + ntx - 1, ntx), lax.rem(tx + 1, ntx)
    far = lax.rem(tx + 2 * core - 1 + ntx, ntx)
    mate = tx + 1 - 2 * core
    targets = (
        (up, tx),
        (up, tx),
        (down, tx),
        (down, tx),
        (ty, left),
        (ty, right),
        (up, far),
        (down, far),
        (ty, mate),
        (ty, mate),
    )
    has_up, has_down, has_left, has_right = ty > 0, ty < nty - 1, tx > 0, tx < ntx - 1
    has_far = ((core == 0) & has_left) | ((core == 1) & has_right)
    sends = (
        has_up,
        has_up,
        has_down,
        has_down,
        has_left,
        has_right,
        has_up & has_far,
        has_down & has_far,
        has_up,
        has_down,
    )
    gets = (
        has_down,
        has_down,
        has_up,
        has_up,
        has_right,
        has_left,
        has_down & has_far,
        has_up & has_far,
        has_up,
        has_down,
    )

    odd = lax.rem(ty, 2)
    partner = ty + 1 - 2 * odd
    last = slices - 1

    def diverted(row):
        rings = jnp.where(lax.rem(row, 2) == 0, row, nty - 1 - row) // 2
        return slices * rings // (nty // 2)

    mine, theirs = diverted(ty), diverted(partner)
    final = jnp.clip(ty + 2 - 4 * odd, 0, nty - 1)
    behind = jnp.clip(ty - 2 + 4 * odd, 0, nty - 1)
    served = (behind != ty) & (lax.rem(behind, 2) == odd) & (diverted((ty + behind) // 2) > 0)

    def goes(way, s, d):
        order = s if way is halo else last - s
        if d < 4:
            return sends[d] & ((odd == (1 if d < 2 else 0)) | (order >= mine))
        return sends[d]

    def start(way, s, ds):
        for d in ds:
            pl.when(goes(way, s, d))(way(s, d).start)

    def await_arrival(way, s, ds):
        for d in ds:
            pl.when(gets[d])(way(s, d).wait_recv)

    def await_departure(way, s, ds):
        for d in ds:
            pl.when(goes(way, s, d))(way(s, d).wait_send)

    low, mid, high = pl.ds(0, h), pl.ds(h, n), pl.ds(3 * h, h)

    def blk(index):
        return pl.ds(pl.multiple_of(index * h, h), h)

    def remote(src, dst, send_sem, recv_sem, target):
        return pltpu.make_async_remote_copy(
            src_ref=src,
            dst_ref=dst,
            send_sem=send_sem,
            recv_sem=recv_sem,
            device_id=target,
            device_id_type=MESH,
        )

    def halo(s, d):
        top, bottom = pl.ds(0, h), pl.ds(h, h)
        everything = slice(None)
        near, away = 1 - core, core
        src, dst = (
            (obj.at[s, :, top, blk(near)], pad.at[s, :, high, blk(1 + near)]),
            (obj.at[s, :, top, blk(away)], pad.at[s, :, high, blk(1 + away)]),
            (obj.at[s, :, bottom, blk(near)], pad.at[s, :, low, blk(1 + near)]),
            (obj.at[s, :, bottom, blk(away)], pad.at[s, :, low, blk(1 + away)]),
            (obj.at[s, :, everything, top], pad.at[s, :, mid, high]),
            (obj.at[s, :, everything, bottom], pad.at[s, :, mid, low]),
            (obj.at[s, :, top, blk(core)], pad.at[s, :, high, blk(3 * (1 - core))]),
            (obj.at[s, :, bottom, blk(core)], pad.at[s, :, low, blk(3 * (1 - core))]),
            (pad.at[s, :, low, blk(1 + near)], pad.at[s, :, low, blk(3 * core)]),
            (pad.at[s, :, high, blk(1 + near)], pad.at[s, :, high, blk(3 * core)]),
        )[d]
        return remote(src, dst, halo_send.at[s, d], halo_recv.at[s, d], targets[d])

    def back(s, d):
        near, away = 1 - core, core
        src, dst = (
            (gpad.at[s, :, low, blk(1 + near)], land_r.at[s, 0, :, :, blk(near)]),
            (gpad.at[s, :, low, blk(1 + away)], land_r.at[s, 0, :, :, blk(away)]),
            (gpad.at[s, :, high, blk(1 + near)], land_r.at[s, 1, :, :, blk(near)]),
            (gpad.at[s, :, high, blk(1 + away)], land_r.at[s, 1, :, :, blk(away)]),
            (gpad.at[s, :, mid, low], land_c.at[s, 0]),
            (gpad.at[s, :, mid, high], land_c.at[s, 1]),
            (gpad.at[s, :, low, blk(3 * core)], land_d.at[s, 0]),
            (gpad.at[s, :, high, blk(3 * core)], land_d.at[s, 1]),
            (gpad.at[s, :, low, blk(3 * (1 - core))], land_m.at[s, 0]),
            (gpad.at[s, :, high, blk(3 * (1 - core))], land_m.at[s, 1]),
        )[d]
        return remote(src, dst, grad_send.at[s, d], grad_recv.at[s, d], targets[d])

    def to_partner(way, s):
        src, phase_index = (obj.at[s, :, blk(odd), :], 0) if way is halo else (gpad.at[s, :, blk(3 * odd), mid], 1)
        return remote(
            src,
            stage.at[phase_index, s],
            first_send.at[phase_index, s],
            first_recv.at[phase_index, s],
            (partner, tx),
        )

    def to_final(way, s, e):
        half = (1 - core, core)[e]
        d = 2 * (1 - odd) + e
        if way is halo:
            dst, arrival, phase_index = pad.at[s, :, blk(3 * odd), blk(1 + half)], halo_recv.at[s, d], 0
        else:
            dst, arrival, phase_index = land_r.at[s, 1 - odd, :, :, blk(half)], grad_recv.at[s, d], 1
        return remote(
            stage.at[phase_index, s, :, :, blk(half)], dst, second_send.at[phase_index, s, e], arrival, (final, tx)
        )

    def divert(way, s):
        pl.when((s if way is halo else last - s) < mine)(to_partner(way, s).start)

    def relay(way, s):
        @pl.when((s if way is halo else last - s) < theirs)
        def _():
            to_partner(way, s).wait_recv()
            for e in range(2):
                to_final(way, s, e).start()

    def settle(way, s):
        await_departure(way, s, range(10))
        order = s if way is halo else last - s
        pl.when(order < mine)(to_partner(way, s).wait_send)

        @pl.when(order < theirs)
        def _():
            for e in range(2):
                to_final(way, s, e).wait_send()

    own = [
        pltpu.make_async_copy(src, dst, own_sem.at[index])
        for index, (src, dst) in enumerate(
            ((dft_in, dft), (probe_in, probe), (phase_in, phase), (obj, pad.at[:, :, mid, mid]), (inten_in, inten))
        )
    ]

    barrier = pltpu.get_barrier_semaphore()
    for d in (0, 2, 4, 5, 6, 7):

        @pl.when(sends[d])
        def _(d=d):
            pl.semaphore_signal(barrier, inc=1, device_id=targets[d], device_id_type=MESH)

    @pl.when(served)
    def _():
        pl.semaphore_signal(barrier, inc=1, device_id=(behind, tx), device_id_type=MESH)

    expected = [sends[d] for d in (0, 2, 4, 5, 6, 7)] + [theirs > 0]
    pl.semaphore_wait(barrier, sum(there.astype(jnp.int32) for there in expected))

    def ask(s):
        start(halo, s, (4, 5, 6, 7))
        divert(halo, s)
        start(halo, s, (0, 2, 1, 3))

    ask(0)
    for copy in own:
        copy.start()

    def corner(k):
        return off[0, k] - (ty * n - h), off[1, k] - (tx * n - h)

    def masks(k, r):
        a, b = corner(k)
        row = lax.broadcasted_iota(jnp.int32, (ROWS, n), 0) + r >= a
        col = lax.broadcasted_iota(jnp.int32, (ROWS, n), 1) >= b
        return row, col

    chunks = range(0, n, ROWS)

    for copy in own[:3]:
        copy.wait()
    for r in chunks:
        kern[0, r : r + ROWS, :] = jnp.cos(phase[r : r + ROWS, :])
        kern[1, r : r + ROWS, :] = jnp.sin(phase[r : r + ROWS, :])

    def prepare(k, carry):
        a, b = corner(k)
        for axis, shift, table, sign in (
            (1, a, tl, -1.0),
            (0, a, tle, 1.0),
            (0, b, tr, 1.0),
            (1, b, tre, -1.0),
        ):
            real = pltpu.roll(dft[0], shift, axis).astype(BF16)
            imag = pltpu.roll(dft[1], shift, axis)
            table[k, 0:n, 0:n] = real
            table[k, n:, n:] = real
            table[k, 0:n, n:] = (sign * imag).astype(BF16)
            table[k, n:, 0:n] = (-sign * imag).astype(BF16)
        for part in range(2):
            moved = pltpu.roll(pltpu.roll(probe[part], a, 0), b, 1)
            wave[k, 0, :, part * n : (part + 1) * n] = moved
        return carry

    lax.fori_loop(0, slots, prepare, 0)
    ask(1)
    for copy in own[3:]:
        copy.wait()

    def illuminate(s, k):
        for r in chunks:
            row, col = masks(k, r)
            rows = slice(r, r + ROWS)
            below = slice(n + r, n + r + ROWS)
            parts = []
            for part in range(2):
                value = jnp.where(
                    row,
                    jnp.where(col, pad[s, part, rows, 0:n].astype(F32), pad[s, part, rows, n:].astype(F32)),
                    jnp.where(col, pad[s, part, below, 0:n].astype(F32), pad[s, part, below, n:].astype(F32)),
                )
                patch[k, s, part, rows, :] = value.astype(BF16)
                parts.append(value)
            pr, pi = parts
            wr, wi = wave[k, s, rows, 0:n], wave[k, s, rows, n:]
            ub[k, rows, :] = (wr * pr - wi * pi).astype(BF16)
            ub[k, below, :] = (wr * pi + wi * pr).astype(BF16)

    def left_of(k, table):
        mb[k, :, 0:n] = dot(table[k, 0:n, :], ub[k]).astype(BF16)
        mb[k, :, n:] = dot(table[k, n:, :], ub[k]).astype(BF16)

    def propagate(k):
        for r in chunks:
            rows = slice(r, r + ROWS)
            below = slice(n + r, n + r + ROWS)
            kr, ki = kern[0, rows, :], kern[1, rows, :]
            xr, xi = xb[k, rows, 0:n], xb[k, rows, n:]
            ub[k, rows, :] = (kr * xr - ki * xi).astype(BF16)
            ub[k, below, :] = (kr * xi + ki * xr).astype(BF16)

    def residual(k):
        weight = live[k].astype(F32)
        for r in chunks:
            rows = slice(r, r + ROWS)
            er, ei = xb[k, rows, 0:n], xb[k, rows, n:]
            resid = (er * er + ei * ei - inten[k, rows, :]) * weight
            scale = 2.0 * weight * resid
            ct[k, rows, 0:n] = (scale * er).astype(BF16)
            ct[k, rows, n:] = (scale * ei).astype(BF16)

    def right_adjoint(k, table):
        yb[k, 0:n, :] = dot(ct[k], table[k, :, 0:n]).astype(BF16)
        yb[k, n:, :] = dot(ct[k], table[k, :, n:]).astype(BF16)

    def left_adjoint(k, table):
        zb[k] = dot(table[k], yb[k]).astype(BF16)

    def gradient(s, k, onward):
        for r in chunks:
            rows = slice(r, r + ROWS)
            below = slice(n + r, n + r + ROWS)
            zr, zi = zb[k, rows, :].astype(F32), zb[k, below, :].astype(F32)
            wr, wi = wave[k, s, rows, 0:n], wave[k, s, rows, n:]
            gc[k, 0, rows, :] = zr * wr + zi * wi
            gc[k, 1, rows, :] = zi * wr - zr * wi
            if onward:
                pr, pi = patch[k, s, 0, rows, :].astype(F32), patch[k, s, 1, rows, :].astype(F32)
                ct[k, rows, 0:n] = (zr * pr + zi * pi).astype(BF16)
                ct[k, rows, n:] = (zi * pr - zr * pi).astype(BF16)

    def propagate_adjoint(k):
        for r in chunks:
            rows = slice(r, r + ROWS)
            below = slice(n + r, n + r + ROWS)
            zr, zi = zb[k, rows, :].astype(F32), zb[k, below, :].astype(F32)
            kr, ki = kern[0, rows, :], kern[1, rows, :]
            ct[k, rows, 0:n] = (kr * zr + ki * zi).astype(BF16)
            ct[k, rows, n:] = (kr * zi - ki * zr).astype(BF16)

    def every(stage, *operands):
        for k in range(slots):
            stage(k, *operands)

    def arrive(s):
        relay(halo, s)
        await_arrival(halo, s, (0, 2))
        start(halo, s, (8, 9))
        await_arrival(halo, s, (1, 3, 4, 5, 6, 7))
        if not isinstance(s, int):
            pl.when(s + 2 < slices)(lambda: ask(s + 2))
        await_arrival(halo, s, (8, 9))

    def forward(s, carry):
        arrive(s)
        for k in range(slots):
            illuminate(s, k)
        every(left_of, tl)
        for k in range(slots):
            xb[k] = dot(mb[k], tr[k])
        every(propagate)
        every(left_of, tle)
        for k in range(slots):
            wave[k, s + 1] = dot(mb[k], tre[k])
        return carry

    lax.fori_loop(0, last, forward, 0)
    arrive(last)

    def tops(s):
        for d, rows in ((0, low), (1, high)):

            @pl.when(gets[8 + d])
            def _(d=d, rows=rows):
                back(s, 8 + d).wait_recv()
                for part in range(2):
                    place = (s, part, rows, blk(2 - core))
                    total = gpad[place].astype(F32) + land_m[s, d, part].astype(F32)
                    gpad[place] = total.astype(BF16)
                start(back, s, (2 * d,))

        divert(back, s)

    def combine(s):
        for part in range(2):
            for r in chunks:
                rows = slice(r, r + ROWS)
                sums = [[None, None], [None, None]]
                for k in range(slots):
                    row, col = masks(k, r)
                    value = gc[k, part, rows, :]
                    zero = jnp.zeros_like(value)
                    for p in range(2):
                        kept = jnp.where(row, value, zero) if p == 0 else jnp.where(row, zero, value)
                        for q in range(2):
                            term = jnp.where(col, kept, zero) if q == 0 else jnp.where(col, zero, kept)
                            sums[p][q] = term if k == 0 else sums[p][q] + term
                for p in range(2):
                    start = p * n + r
                    inside = h <= start < h + n
                    for q in range(2):
                        if not inside:
                            gpad[s, part, start : start + ROWS, q * n : (q + 1) * n] = sums[p][q].astype(BF16)
                            continue
                        place = slice(start - h, start - h + ROWS)
                        if q == 0:
                            gpad[s, part, start : start + ROWS, 0:h] = sums[p][q][:, 0:h].astype(BF16)
                            out[s, part, place, 0:h] = sums[p][q][:, h:]
                        else:
                            out[s, part, place, h:] = sums[p][q][:, 0:h]
                            gpad[s, part, start : start + ROWS, 3 * h :] = sums[p][q][:, h:].astype(BF16)

    def sides(s):
        start(back, s, (8, 9, 4, 5, 6, 7))

    for k in range(slots):
        illuminate(last, k)
    every(left_of, tl)
    for k in range(slots):
        xb[k] = dot(mb[k], tr[k])
    every(residual)

    def backward(t, carry):
        s = last - t
        every(right_adjoint, tre)
        every(left_adjoint, tle)
        for k in range(slots):
            gradient(s, k, True)
        combine(s)
        sides(s)
        start(back, s, (1, 3))
        every(right_adjoint, tr)
        tops(s)

        @pl.when(t > 0)
        def _():
            relay(back, s + 1)

        every(left_adjoint, tl)
        every(propagate_adjoint)
        return carry

    lax.fori_loop(0, last, backward, 0)
    every(right_adjoint, tre)
    every(left_adjoint, tle)
    for k in range(slots):
        gradient(0, k, False)
    combine(0)
    sides(0)
    start(back, 0, (1, 3))
    relay(back, 1)
    tops(0)

    def collect(t, carry):
        s = last - t
        whole, first, second = pl.ds(0, n), pl.ds(0, h), pl.ds(h, h)
        for ds, landed, rows, cols in (
            ((4,), land_c.at[s, 0], whole, second),
            ((5,), land_c.at[s, 1], whole, first),
            ((6,), land_d.at[s, 0], second, blk(core)),
            ((7,), land_d.at[s, 1], first, blk(core)),
            ((0, 1), land_r.at[s, 0], second, whole),
            ((2, 3), land_r.at[s, 1], first, whole),
        ):

            @pl.when(gets[ds[0]])
            def _(ds=ds, landed=landed, rows=rows, cols=cols):
                for d in ds:
                    back(s, d).wait_recv()
                for part in range(2):
                    place = (s, part, rows, cols)
                    out[place] = out[place] + landed[part].astype(F32)

        return carry

    lax.fori_loop(0, slices, collect, 0)

    def drain(s, carry):
        settle(halo, s)
        settle(back, s)
        return carry

    lax.fori_loop(0, slices, drain, 0)


def per_device(grid, object_slices, probe_wave, intensity, offsets, live_slots, prop_phase):
    slices, _, n, _ = object_slices.shape
    slots = intensity.shape[0]
    h = n // 2
    vmem, smem = pl.BlockSpec(memory_space=pltpu.VMEM), pl.BlockSpec(memory_space=pltpu.SMEM)
    table = pltpu.VMEM((slots, 2 * n, 2 * n), BF16)
    return pl.pallas_call(
        functools.partial(kernel, grid),
        out_shape=pltpu.VMEM(object_slices.shape, F32),
        in_specs=[smem, smem] + [pl.BlockSpec(memory_space=pl.ANY)] * 5,
        out_specs=vmem,
        scratch_shapes=[
            pltpu.VMEM(probe_wave.shape, F32),
            pltpu.VMEM(intensity.shape, F32),
            pltpu.VMEM(prop_phase.shape, F32),
            pltpu.VMEM((2, n, n), F32),
            pltpu.VMEM((slices, 2, 2 * n, 2 * n), BF16),
            pltpu.VMEM((slices, 2, 2 * n, 2 * n), BF16),
            pltpu.VMEM((slots, slices, 2, n, n), BF16),
            pltpu.VMEM((slots, slices, n, 2 * n), F32),
            table,
            table,
            table,
            table,
            pltpu.VMEM((2, n, n), F32),
            pltpu.VMEM((slots, 2 * n, n), BF16),
            pltpu.VMEM((slots, n, 2 * n), BF16),
            pltpu.VMEM((slots, n, 2 * n), F32),
            pltpu.VMEM((slots, n, 2 * n), BF16),
            pltpu.VMEM((slots, 2 * n, n), BF16),
            pltpu.VMEM((slots, 2 * n, n), BF16),
            pltpu.VMEM((slots, 2, n, n), F32),
            pltpu.VMEM((slices, 2, 2, h, n), BF16),
            pltpu.VMEM((slices, 2, 2, n, h), BF16),
            pltpu.VMEM((slices, 2, 2, h, h), BF16),
            pltpu.VMEM((slices, 2, 2, h, h), BF16),
            pltpu.SemaphoreType.DMA((slices, 10)),
            pltpu.SemaphoreType.DMA((slices, 10)),
            pltpu.SemaphoreType.DMA((slices, 10)),
            pltpu.SemaphoreType.DMA((slices, 10)),
            pltpu.SemaphoreType.DMA((5,)),
            pltpu.VMEM((2, slices, 2, h, n), BF16),
            pltpu.SemaphoreType.DMA((2, slices)),
            pltpu.SemaphoreType.DMA((2, slices)),
            pltpu.SemaphoreType.DMA((2, slices, 2)),
        ],
        compiler_params=pltpu.CompilerParams(
            collective_id=0, has_side_effects=True, vmem_limit_bytes=56 * 1024 * 1024
        ),
    )(
        offsets.T,
        live_slots,
        object_slices,
        probe_wave,
        intensity,
        prop_phase,
        jnp.asarray(dft_matrix(n)),
    )


def solution(mesh):
    in_specs = (
        P(None, None, "ty", "tx"),
        P(),
        P(("ty", "tx"), None, None),
        P(("ty", "tx"), None),
        P(("ty", "tx")),
        P(),
    )
    out_specs = P(None, None, "ty", "tx")
    grid = (mesh.shape["ty"], mesh.shape["tx"])
    return jax.shard_map(
        functools.partial(per_device, grid),
        mesh=mesh,
        in_specs=in_specs,
        out_specs=out_specs,
        check_vma=False,
    )
```

```python
import functools
import math

import jax
import jax.numpy as jnp
import numpy as np
from jax import lax
from jax.experimental import pallas as pl
from jax.experimental.pallas import tpu as pltpu
from jax.sharding import PartitionSpec as P

MESH = pl.DeviceIdType.MESH
BF16 = jnp.bfloat16
F32 = jnp.float32
ROWS = 64


def dft_matrix(side):
    index = np.arange(side)
    angle = (index[:, None] * index[None, :] % side) * (2.0 * math.pi / side)
    parts = np.stack([np.cos(angle), -np.sin(angle)]) / math.sqrt(side)
    return parts.astype(np.float32).astype(jnp.bfloat16).astype(np.float32)


def dot(first, second):
    return jnp.dot(first, second, preferred_element_type=F32)


def kernel(
    grid,
    off,
    live,
    obj,
    probe_in,
    inten_in,
    phase_in,
    dft_in,
    out,
    probe,
    inten,
    phase,
    dft,
    pad,
    gpad,
    patch,
    wave,
    tl,
    tle,
    tr,
    tre,
    kern,
    ub,
    mb,
    xb,
    ct,
    yb,
    zb,
    gc,
    land_r,
    land_c,
    land_d,
    land_m,
    halo_send,
    halo_recv,
    grad_send,
    grad_recv,
    own_sem,
    stage,
    first_send,
    first_recv,
    second_send,
):
    nty, ntx = grid
    slices, _, n, _ = obj.shape
    slots = inten.shape[0]
    h = n // 2
    ty, tx = lax.axis_index("ty"), lax.axis_index("tx")
    core = lax.rem(tx, 2)
    up, down = lax.rem(ty + nty - 1, nty), lax.rem(ty + 1, nty)
    left, right = lax.rem(tx + ntx - 1, ntx), lax.rem(tx + 1, ntx)
    far = lax.rem(tx + 2 * core - 1 + ntx, ntx)
    mate = tx + 1 - 2 * core
    targets = (
        (up, tx),
        (up, tx),
        (down, tx),
        (down, tx),
        (ty, left),
        (ty, right),
        (up, far),
        (down, far),
        (ty, mate),
        (ty, mate),
    )
    has_up, has_down, has_left, has_right = ty > 0, ty < nty - 1, tx > 0, tx < ntx - 1
    has_far = ((core == 0) & has_left) | ((core == 1) & has_right)
    sends = (
        has_up,
        has_up,
        has_down,
        has_down,
        has_left,
        has_right,
        has_up & has_far,
        has_down & has_far,
        has_up,
        has_down,
    )
    gets = (
        has_down,
        has_down,
        has_up,
        has_up,
        has_right,
        has_left,
        has_down & has_far,
        has_up & has_far,
        has_up,
        has_down,
    )

    odd = lax.rem(ty, 2)
    partner = ty + 1 - 2 * odd
    last = slices - 1

    def diverted(row):
        rings = jnp.where(lax.rem(row, 2) == 0, row, nty - 1 - row) // 2
        return slices * rings // (nty // 2)

    mine, theirs = diverted(ty), diverted(partner)
    final = jnp.clip(ty + 2 - 4 * odd, 0, nty - 1)
    behind = jnp.clip(ty - 2 + 4 * odd, 0, nty - 1)
    served = (behind != ty) & (lax.rem(behind, 2) == odd) & (diverted((ty + behind) // 2) > 0)

    def goes(way, s, d):
        order = s if way is halo else last - s
        if d < 4:
            return sends[d] & ((odd == (1 if d < 2 else 0)) | (order >= mine))
        return sends[d]

    def start(way, s, ds):
        for d in ds:
            pl.when(goes(way, s, d))(way(s, d).start)

    def await_arrival(way, s, ds):
        for d in ds:
            pl.when(gets[d])(way(s, d).wait_recv)

    def await_departure(way, s, ds):
        for d in ds:
            pl.when(goes(way, s, d))(way(s, d).wait_send)

    low, mid, high = pl.ds(0, h), pl.ds(h, n), pl.ds(3 * h, h)

    def blk(index):
        return pl.ds(pl.multiple_of(index * h, h), h)

    def remote(src, dst, send_sem, recv_sem, target):
        return pltpu.make_async_remote_copy(
            src_ref=src,
            dst_ref=dst,
            send_sem=send_sem,
            recv_sem=recv_sem,
            device_id=target,
            device_id_type=MESH,
        )

    def halo(s, d):
        top, bottom = pl.ds(0, h), pl.ds(h, h)
        everything = slice(None)
        near, away = 1 - core, core
        src, dst = (
            (obj.at[s, :, top, blk(near)], pad.at[s, :, high, blk(1 + near)]),
            (obj.at[s, :, top, blk(away)], pad.at[s, :, high, blk(1 + away)]),
            (obj.at[s, :, bottom, blk(near)], pad.at[s, :, low, blk(1 + near)]),
            (obj.at[s, :, bottom, blk(away)], pad.at[s, :, low, blk(1 + away)]),
            (obj.at[s, :, everything, top], pad.at[s, :, mid, high]),
            (obj.at[s, :, everything, bottom], pad.at[s, :, mid, low]),
            (obj.at[s, :, top, blk(core)], pad.at[s, :, high, blk(3 * (1 - core))]),
            (obj.at[s, :, bottom, blk(core)], pad.at[s, :, low, blk(3 * (1 - core))]),
            (pad.at[s, :, low, blk(1 + near)], pad.at[s, :, low, blk(3 * core)]),
            (pad.at[s, :, high, blk(1 + near)], pad.at[s, :, high, blk(3 * core)]),
        )[d]
        return remote(src, dst, halo_send.at[s, d], halo_recv.at[s, d], targets[d])

    def back(s, d):
        near, away = 1 - core, core
        src, dst = (
            (gpad.at[s, :, low, blk(1 + near)], land_r.at[s, 0, :, :, blk(near)]),
            (gpad.at[s, :, low, blk(1 + away)], land_r.at[s, 0, :, :, blk(away)]),
            (gpad.at[s, :, high, blk(1 + near)], land_r.at[s, 1, :, :, blk(near)]),
            (gpad.at[s, :, high, blk(1 + away)], land_r.at[s, 1, :, :, blk(away)]),
            (gpad.at[s, :, mid, low], land_c.at[s, 0]),
            (gpad.at[s, :, mid, high], land_c.at[s, 1]),
            (gpad.at[s, :, low, blk(3 * core)], land_d.at[s, 0]),
            (gpad.at[s, :, high, blk(3 * core)], land_d.at[s, 1]),
            (gpad.at[s, :, low, blk(3 * (1 - core))], land_m.at[s, 0]),
            (gpad.at[s, :, high, blk(3 * (1 - core))], land_m.at[s, 1]),
        )[d]
        return remote(src, dst, grad_send.at[s, d], grad_recv.at[s, d], targets[d])

    def to_partner(way, s):
        src, phase_index = (obj.at[s, :, blk(odd), :], 0) if way is halo else (gpad.at[s, :, blk(3 * odd), mid], 1)
        return remote(
            src,
            stage.at[phase_index, s],
            first_send.at[phase_index, s],
            first_recv.at[phase_index, s],
            (partner, tx),
        )

    def to_final(way, s, e):
        half = (1 - core, core)[e]
        d = 2 * (1 - odd) + e
        if way is halo:
            dst, arrival, phase_index = pad.at[s, :, blk(3 * odd), blk(1 + half)], halo_recv.at[s, d], 0
        else:
            dst, arrival, phase_index = land_r.at[s, 1 - odd, :, :, blk(half)], grad_recv.at[s, d], 1
        return remote(
            stage.at[phase_index, s, :, :, blk(half)], dst, second_send.at[phase_index, s, e], arrival, (final, tx)
        )

    def divert(way, s):
        pl.when((s if way is halo else last - s) < mine)(to_partner(way, s).start)

    def relay(way, s):
        @pl.when((s if way is halo else last - s) < theirs)
        def _():
            to_partner(way, s).wait_recv()
            for e in range(2):
                to_final(way, s, e).start()

    def settle(way, s):
        await_departure(way, s, range(10))
        order = s if way is halo else last - s
        pl.when(order < mine)(to_partner(way, s).wait_send)

        @pl.when(order < theirs)
        def _():
            for e in range(2):
                to_final(way, s, e).wait_send()

    own = [
        pltpu.make_async_copy(src, dst, own_sem.at[index])
        for index, (src, dst) in enumerate(
            ((dft_in, dft), (probe_in, probe), (phase_in, phase), (obj, pad.at[:, :, mid, mid]), (inten_in, inten))
        )
    ]

    barrier = pltpu.get_barrier_semaphore()
    for d in (0, 2, 4, 5, 6, 7):

        @pl.when(sends[d])
        def _(d=d):
            pl.semaphore_signal(barrier, inc=1, device_id=targets[d], device_id_type=MESH)

    @pl.when(served)
    def _():
        pl.semaphore_signal(barrier, inc=1, device_id=(behind, tx), device_id_type=MESH)

    expected = [sends[d] for d in (0, 2, 4, 5, 6, 7)] + [theirs > 0]
    pl.semaphore_wait(barrier, sum(there.astype(jnp.int32) for there in expected))

    def ask(s):
        start(halo, s, (4, 5, 6, 7))
        divert(halo, s)
        start(halo, s, (0, 2, 1, 3))

    ask(0)
    for copy in own:
        copy.start()

    def corner(k):
        return off[0, k] - (ty * n - h), off[1, k] - (tx * n - h)

    def masks(k, r):
        a, b = corner(k)
        row = lax.broadcasted_iota(jnp.int32, (ROWS, n), 0) + r >= a
        col = lax.broadcasted_iota(jnp.int32, (ROWS, n), 1) >= b
        return row, col

    chunks = range(0, n, ROWS)

    for copy in own[:3]:
        copy.wait()
    for r in chunks:
        kern[0, r : r + ROWS, :] = jnp.cos(phase[r : r + ROWS, :])
        kern[1, r : r + ROWS, :] = jnp.sin(phase[r : r + ROWS, :])

    def prepare(k, carry):
        a, b = corner(k)
        for axis, shift, table, sign in (
            (1, a, tl, -1.0),
            (0, a, tle, 1.0),
            (0, b, tr, 1.0),
            (1, b, tre, -1.0),
        ):
            real = pltpu.roll(dft[0], shift, axis).astype(BF16)
            imag = pltpu.roll(dft[1], shift, axis)
            table[k, 0:n, 0:n] = real
            table[k, n:, n:] = real
            table[k, 0:n, n:] = (sign * imag).astype(BF16)
            table[k, n:, 0:n] = (-sign * imag).astype(BF16)
        for part in range(2):
            moved = pltpu.roll(pltpu.roll(probe[part], a, 0), b, 1)
            wave[k, 0, :, part * n : (part + 1) * n] = moved
        return carry

    lax.fori_loop(0, slots, prepare, 0)
    ask(1)
    for copy in own[3:]:
        copy.wait()

    def illuminate(s, k):
        for r in chunks:
            row, col = masks(k, r)
            rows = slice(r, r + ROWS)
            below = slice(n + r, n + r + ROWS)
            parts = []
            for part in range(2):
                value = jnp.where(
                    row,
                    jnp.where(col, pad[s, part, rows, 0:n].astype(F32), pad[s, part, rows, n:].astype(F32)),
                    jnp.where(col, pad[s, part, below, 0:n].astype(F32), pad[s, part, below, n:].astype(F32)),
                )
                patch[k, s, part, rows, :] = value.astype(BF16)
                parts.append(value)
            pr, pi = parts
            wr, wi = wave[k, s, rows, 0:n], wave[k, s, rows, n:]
            ub[k, rows, :] = (wr * pr - wi * pi).astype(BF16)
            ub[k, below, :] = (wr * pi + wi * pr).astype(BF16)

    def left_of(k, table):
        mb[k, :, 0:n] = dot(table[k, 0:n, :], ub[k]).astype(BF16)
        mb[k, :, n:] = dot(table[k, n:, :], ub[k]).astype(BF16)

    def propagate(k):
        for r in chunks:
            rows = slice(r, r + ROWS)
            below = slice(n + r, n + r + ROWS)
            kr, ki = kern[0, rows, :], kern[1, rows, :]
            xr, xi = xb[k, rows, 0:n], xb[k, rows, n:]
            ub[k, rows, :] = (kr * xr - ki * xi).astype(BF16)
            ub[k, below, :] = (kr * xi + ki * xr).astype(BF16)

    def residual(k):
        weight = live[k].astype(F32)
        for r in chunks:
            rows = slice(r, r + ROWS)
            er, ei = xb[k, rows, 0:n], xb[k, rows, n:]
            resid = (er * er + ei * ei - inten[k, rows, :]) * weight
            scale = 2.0 * weight * resid
            ct[k, rows, 0:n] = (scale * er).astype(BF16)
            ct[k, rows, n:] = (scale * ei).astype(BF16)

    def right_adjoint(k, table):
        yb[k, 0:n, :] = dot(ct[k], table[k, :, 0:n]).astype(BF16)
        yb[k, n:, :] = dot(ct[k], table[k, :, n:]).astype(BF16)

    def left_adjoint(k, table):
        zb[k] = dot(table[k], yb[k]).astype(BF16)

    def gradient(s, k, onward):
        for r in chunks:
            rows = slice(r, r + ROWS)
            below = slice(n + r, n + r + ROWS)
            zr, zi = zb[k, rows, :].astype(F32), zb[k, below, :].astype(F32)
            wr, wi = wave[k, s, rows, 0:n], wave[k, s, rows, n:]
            gc[k, 0, rows, :] = zr * wr + zi * wi
            gc[k, 1, rows, :] = zi * wr - zr * wi
            if onward:
                pr, pi = patch[k, s, 0, rows, :].astype(F32), patch[k, s, 1, rows, :].astype(F32)
                ct[k, rows, 0:n] = (zr * pr + zi * pi).astype(BF16)
                ct[k, rows, n:] = (zi * pr - zr * pi).astype(BF16)

    def propagate_adjoint(k):
        for r in chunks:
            rows = slice(r, r + ROWS)
            below = slice(n + r, n + r + ROWS)
            zr, zi = zb[k, rows, :].astype(F32), zb[k, below, :].astype(F32)
            kr, ki = kern[0, rows, :], kern[1, rows, :]
            ct[k, rows, 0:n] = (kr * zr + ki * zi).astype(BF16)
            ct[k, rows, n:] = (kr * zi - ki * zr).astype(BF16)

    def every(stage, *operands):
        for k in range(slots):
            stage(k, *operands)

    def arrive(s):
        relay(halo, s)
        await_arrival(halo, s, (0, 2))
        start(halo, s, (8, 9))
        await_arrival(halo, s, (1, 3, 4, 5, 6, 7))
        if not isinstance(s, int):
            pl.when(s + 2 < slices)(lambda: ask(s + 2))
        await_arrival(halo, s, (8, 9))

    def forward(s, carry):
        arrive(s)
        for k in range(slots):
            illuminate(s, k)
        every(left_of, tl)
        for k in range(slots):
            xb[k] = dot(mb[k], tr[k])
        every(propagate)
        every(left_of, tle)
        for k in range(slots):
            wave[k, s + 1] = dot(mb[k], tre[k])
        return carry

    lax.fori_loop(0, last, forward, 0)
    arrive(last)

    def tops(s):
        for d, rows in ((0, low), (1, high)):

            @pl.when(gets[8 + d])
            def _(d=d, rows=rows):
                back(s, 8 + d).wait_recv()
                for part in range(2):
                    place = (s, part, rows, blk(2 - core))
                    total = gpad[place].astype(F32) + land_m[s, d, part].astype(F32)
                    gpad[place] = total.astype(BF16)
                start(back, s, (2 * d,))

        divert(back, s)

    def combine(s):
        for part in range(2):
            for r in chunks:
                rows = slice(r, r + ROWS)
                sums = [[None, None], [None, None]]
                for k in range(slots):
                    row, col = masks(k, r)
                    value = gc[k, part, rows, :]
                    zero = jnp.zeros_like(value)
                    for p in range(2):
                        kept = jnp.where(row, value, zero) if p == 0 else jnp.where(row, zero, value)
                        for q in range(2):
                            term = jnp.where(col, kept, zero) if q == 0 else jnp.where(col, zero, kept)
                            sums[p][q] = term if k == 0 else sums[p][q] + term
                for p in range(2):
                    start = p * n + r
                    inside = h <= start < h + n
                    for q in range(2):
                        if not inside:
                            gpad[s, part, start : start + ROWS, q * n : (q + 1) * n] = sums[p][q].astype(BF16)
                            continue
                        place = slice(start - h, start - h + ROWS)
                        if q == 0:
                            gpad[s, part, start : start + ROWS, 0:h] = sums[p][q][:, 0:h].astype(BF16)
                            out[s, part, place, 0:h] = sums[p][q][:, h:]
                        else:
                            out[s, part, place, h:] = sums[p][q][:, 0:h]
                            gpad[s, part, start : start + ROWS, 3 * h :] = sums[p][q][:, h:].astype(BF16)

    def sides(s):
        start(back, s, (8, 9, 4, 5, 6, 7))

    for k in range(slots):
        illuminate(last, k)
    every(left_of, tl)
    for k in range(slots):
        xb[k] = dot(mb[k], tr[k])
    every(residual)

    def backward(t, carry):
        s = last - t
        every(right_adjoint, tre)
        every(left_adjoint, tle)
        for k in range(slots):
            gradient(s, k, True)
        combine(s)
        sides(s)
        start(back, s, (1, 3))
        every(right_adjoint, tr)
        tops(s)

        @pl.when(t > 0)
        def _():
            relay(back, s + 1)

        every(left_adjoint, tl)
        every(propagate_adjoint)
        return carry

    lax.fori_loop(0, last, backward, 0)
    every(right_adjoint, tre)
    every(left_adjoint, tle)
    for k in range(slots):
        gradient(0, k, False)
    combine(0)
    sides(0)
    start(back, 0, (1, 3))
    relay(back, 1)
    tops(0)

    def collect(t, carry):
        s = last - t
        whole, first, second = pl.ds(0, n), pl.ds(0, h), pl.ds(h, h)
        for ds, landed, rows, cols in (
            ((4,), land_c.at[s, 0], whole, second),
            ((5,), land_c.at[s, 1], whole, first),
            ((6,), land_d.at[s, 0], second, blk(core)),
            ((7,), land_d.at[s, 1], first, blk(core)),
            ((0, 1), land_r.at[s, 0], second, whole),
            ((2, 3), land_r.at[s, 1], first, whole),
        ):

            @pl.when(gets[ds[0]])
            def _(ds=ds, landed=landed, rows=rows, cols=cols):
                for d in ds:
                    back(s, d).wait_recv()
                for part in range(2):
                    place = (s, part, rows, cols)
                    out[place] = out[place] + landed[part].astype(F32)

        return carry

    lax.fori_loop(0, slices, collect, 0)

    def drain(s, carry):
        settle(halo, s)
        settle(back, s)
        return carry

    lax.fori_loop(0, slices, drain, 0)


def per_device(grid, object_slices, probe_wave, intensity, offsets, live_slots, prop_phase):
    slices, _, n, _ = object_slices.shape
    slots = intensity.shape[0]
    h = n // 2
    vmem, smem = pl.BlockSpec(memory_space=pltpu.VMEM), pl.BlockSpec(memory_space=pltpu.SMEM)
    table = pltpu.VMEM((slots, 2 * n, 2 * n), BF16)
    return pl.pallas_call(
        functools.partial(kernel, grid),
        out_shape=pltpu.VMEM(object_slices.shape, F32),
        in_specs=[smem, smem] + [pl.BlockSpec(memory_space=pl.ANY)] * 5,
        out_specs=vmem,
        scratch_shapes=[
            pltpu.VMEM(probe_wave.shape, F32),
            pltpu.VMEM(intensity.shape, F32),
            pltpu.VMEM(prop_phase.shape, F32),
            pltpu.VMEM((2, n, n), F32),
            pltpu.VMEM((slices, 2, 2 * n, 2 * n), BF16),
            pltpu.VMEM((slices, 2, 2 * n, 2 * n), BF16),
            pltpu.VMEM((slots, slices, 2, n, n), BF16),
            pltpu.VMEM((slots, slices, n, 2 * n), F32),
            table,
            table,
            table,
            table,
            pltpu.VMEM((2, n, n), F32),
            pltpu.VMEM((slots, 2 * n, n), BF16),
            pltpu.VMEM((slots, n, 2 * n), BF16),
            pltpu.VMEM((slots, n, 2 * n), F32),
            pltpu.VMEM((slots, n, 2 * n), BF16),
            pltpu.VMEM((slots, 2 * n, n), BF16),
            pltpu.VMEM((slots, 2 * n, n), BF16),
            pltpu.VMEM((slots, 2, n, n), F32),
            pltpu.VMEM((slices, 2, 2, h, n), BF16),
            pltpu.VMEM((slices, 2, 2, n, h), BF16),
            pltpu.VMEM((slices, 2, 2, h, h), BF16),
            pltpu.VMEM((slices, 2, 2, h, h), BF16),
            pltpu.SemaphoreType.DMA((slices, 10)),
            pltpu.SemaphoreType.DMA((slices, 10)),
            pltpu.SemaphoreType.DMA((slices, 10)),
            pltpu.SemaphoreType.DMA((slices, 10)),
            pltpu.SemaphoreType.DMA((5,)),
            pltpu.VMEM((2, slices, 2, h, n), BF16),
            pltpu.SemaphoreType.DMA((2, slices)),
            pltpu.SemaphoreType.DMA((2, slices)),
            pltpu.SemaphoreType.DMA((2, slices, 2)),
        ],
        compiler_params=pltpu.CompilerParams(
            collective_id=0, has_side_effects=True, vmem_limit_bytes=56 * 1024 * 1024
        ),
    )(
        offsets.T,
        live_slots,
        object_slices,
        probe_wave,
        intensity,
        prop_phase,
        jnp.asarray(dft_matrix(n)),
    )


def solution(mesh):
    in_specs = (
        P(None, None, "ty", "tx"),
        P(),
        P(("ty", "tx"), None, None),
        P(("ty", "tx"), None),
        P(("ty", "tx")),
        P(),
    )
    out_specs = P(None, None, "ty", "tx")
    grid = (mesh.shape["ty"], mesh.shape["tx"])
    return jax.shard_map(
        functools.partial(per_device, grid),
        mesh=mesh,
        in_specs=in_specs,
        out_specs=out_specs,
        check_vma=False,
    )
```
